768 devices in a mesh: grp: 8 (over x, core), dp: 96 (over z, y).
Axes of the slice: x: 4, y: 8, z: 12, core: 2. Of those that a mesh axis runs over, the one named last changes fastest.
Arguments:
- queries: bfloat16 [98304, 256], P(('grp', 'dp')), may hold values from -11 to 11
- item_vecs: bfloat16 [122880, 256], P(('grp', 'dp')), may hold values from -1 to 1
- log_q: bfloat16 [122880], P(('grp', 'dp')), may hold values from -10 to -7
- weights: bfloat16 [98304], P(('grp', 'dp')), may hold values from 0.3 to 12
- item_owner: int32 [122880, 1], P(('grp', 'dp')), may hold values from 0 to 95; in each aligned block of 160 rows (0 to 159, 160 to 319, ...) at most 2 rows name the same one
- item_row: int32 [122880], P(('grp', 'dp')), may hold values from 0 to 1023
Outputs:
- query_grad: bfloat16 [98304, 256], P(('grp', 'dp'))
- table_grad: float32 [786432, 256], P(('grp', 'dp'))
The draws below stay inside these ranges and needn't reach their ends.
Inputs may be any that keep to these rules, and one draw needn't show every extreme that they name: `item_owner`: among the items of one block of 160 rows no owner is named more than 2 times, and in some blocks an owner is named exactly 2 times.
All inputs are finite; a program needn't handle non-finite values.
Results may differ from the reference program's by a relative error of at most 0.012.
Values may be sent and summed in bfloat16 or wider, within the bound.
A program may use at most 32 MiB of HBM per device.

```python
import math
import jax
import jax.numpy as jnp
import numpy as np
from jax import lax

D = 256
B_DEV = 128
M_DEV = 32
ROWS_DEV = 1024
CAP = 2
BATCH = 98304
ITEMS = 122880
TABLE_ROWS = 786432
N_GRP = 8
N_DP = 96


def draw_queries(key, part):
    key = jax.random.fold_in(key, 11)
    devices = BATCH // B_DEV
    result = jnp.clip(0.25 * jax.random.normal(key, (devices, B_DEV, D), jnp.float32), -1.0, 1.0)
    return result.reshape(BATCH, D).astype(jnp.bfloat16)


def draw_item_vecs(key, part):
    key = jax.random.fold_in(key, 12)
    devices = BATCH // B_DEV
    positives = jnp.clip(0.25 * jax.random.normal(key, (devices, B_DEV, D), jnp.float32), -1.0, 1.0)
    other_key = jax.random.fold_in(key, 1)
    negatives = jnp.clip(0.25 * jax.random.normal(other_key, (devices, M_DEV, D), jnp.float32), -1.0, 1.0)
    return jnp.concatenate([positives, negatives], axis=1).reshape(ITEMS, D).astype(jnp.bfloat16)


def draw_log_q(key, part):
    key = jax.random.fold_in(key, 13)
    devices = BATCH // B_DEV
    values = jax.random.uniform(key, (devices, B_DEV + M_DEV), jnp.float32, -10.0, -7.0)
    local = jnp.arange(B_DEV + M_DEV)
    following = (local % 16 == 1) & (local < B_DEV)
    values = jnp.where(following[None, :], jnp.roll(values, 1, axis=1), values)
    return values.reshape(ITEMS).astype(jnp.bfloat16)


def draw_weights(key, part):
    key = jax.random.fold_in(key, 14)
    devices = BATCH // B_DEV
    place = jnp.arange(devices, dtype=jnp.float32) / (devices - 1)
    local = jax.random.uniform(key, (devices, B_DEV), jnp.float32, 0.5, 1.5)
    ramp = 1.0 + 2.0 * place
    return (local * ramp[:, None]).reshape(BATCH).astype(jnp.bfloat16)


def place_ends(values, stream_key, low, largest):
    longest = values.shape.index(max(values.shape))
    spots = []
    for shift in (0, 1):
        where = [jax.random.randint(jax.random.fold_in(stream_key, axis), (), 0, length) for axis, length in enumerate(values.shape)]
        where[longest] = (where[longest] + shift) % values.shape[longest]
        spots.append(tuple(where))
    return values.at[spots[0]].set(low).at[spots[1]].set(largest)


def rank_table(count, lean):
    loads = [(1 << 20) // math.isqrt(standing ** lean) + 1 for standing in range(1, count + 1)]
    deviation = 1 + sum(loads) // (1 << 30)
    return np.cumsum(np.array([max(1, weight // deviation) for weight in loads]))


def ranked_ids(key, shape, number_of, lean):
    table = rank_table(number_of, lean)
    ticket = jax.random.randint(jax.random.fold_in(key, 1), shape, 0, int(table[number_of - 1]))
    grade = jnp.searchsorted(jnp.asarray(table, jnp.int32), ticket, side="right")
    return jax.random.permutation(jax.random.fold_in(key, 2), number_of)[grade].astype(jnp.int32)


def routed_block(own_key, own, number, rows, amount, top, reach, lean):
    sequence = jax.random.permutation(own_key, amount)
    heavy_load, usual = load_shares(amount, rows * top, reach, lean, True), load_shares(amount, rows * top, reach, lean, False)
    places = jnp.arange(amount)

    def named(sizes, offset_by):
        used = int((sizes > 0).sum())
        fixed = max(1, used // 4)
        moved = fixed + (places - fixed + offset_by * (used - fixed)) % max(1, amount - fixed)
        return jnp.zeros((amount,), jnp.int32).at[sequence[jnp.where(places < fixed, places, moved)]].set(jnp.asarray(sizes, jnp.int32))

    sizes = jnp.where(number % 4 == 0, named(heavy_load, number // 4), named(usual, number - number // 4 - 1))
    mixed = jax.random.permutation(jax.random.fold_in(own, 3), amount)
    source_of, taker = mixed[0:amount // 2 * 2:2], mixed[1:amount // 2 * 2:2]
    margin = jnp.minimum(sizes[source_of] - 1, reach - sizes[taker]) // 2
    margin = jnp.where((source_of == sequence[0]) | (taker == sequence[0]) | (sizes[taker] == 0), 0, jnp.maximum(margin, 0))
    moved = jax.random.randint(jax.random.fold_in(own, 4), (amount // 2,), 0, 1 << 20) % (margin + 1)
    sizes = sizes.at[source_of].add(-moved).at[taker].add(moved)
    items = jnp.searchsorted(jnp.cumsum(sizes), jnp.arange(rows * top), side="right").astype(jnp.int32)
    listing = items.reshape(top, rows).T
    listing = listing[jax.random.permutation(jax.random.fold_in(own, 1), rows)]
    offset_by = jax.random.randint(jax.random.fold_in(own, 2), (rows, 1), 0, top)
    return jnp.take_along_axis(listing, (jnp.arange(top)[None, :] + offset_by) % top, axis=1)


def load_shares(count, total, reach, lean, full):
    portions = [(1 << 20) // math.isqrt(grade ** lean) + 1 for grade in range(1, count + 1)]
    largest = reach if full else min(reach, max(-(-total // count), total * portions[0] // sum(portions)))
    least = 1 if total - largest >= count - 1 else 0
    holding, rest = [largest] + [least] * (count - 1), total - largest - least * (count - 1)
    while rest > 0:
        free = [i for i in range(1, count) if holding[i] < largest] or [i for i in range(1, count) if holding[i] < reach]
        whole, remaining = sum([portions[i] for i in free]), rest
        for i in free:
            extra = min(reach - holding[i], max(1, remaining * portions[i] // whole), rest)
            holding[i] = holding[i] + extra
            rest = rest - extra
    return np.array(holding)


def setup_inputs(seed: int = 0) -> dict:
    streams_of = jax.random.split(jax.random.key(seed), 7)
    queries = draw_queries(jax.random.fold_in(streams_of[6], 71), 0)
    item_vecs = draw_item_vecs(jax.random.fold_in(streams_of[6], 71), 0)
    log_q = draw_log_q(jax.random.fold_in(streams_of[6], 71), 0)
    weights = draw_weights(jax.random.fold_in(streams_of[6], 71), 0)
    item_owner_keys = jax.random.split(jax.random.fold_in(streams_of[4], 1), ITEMS // (B_DEV + M_DEV))
    item_owner_turns = jax.random.permutation(jax.random.fold_in(streams_of[4], 3), ITEMS // (B_DEV + M_DEV))
    item_owner = jax.vmap(lambda own, number: routed_block(jax.random.fold_in(streams_of[4], 2), own, number, B_DEV + M_DEV, N_DP, 1, CAP, 2))(item_owner_keys, item_owner_turns).reshape((ITEMS, 1))
    item_row = place_ends(ranked_ids(streams_of[5], (ITEMS,), ROWS_DEV, 2), jax.random.fold_in(streams_of[5], 3), 0, ROWS_DEV - 1).astype(jnp.int32)
    return dict(queries=queries, item_vecs=item_vecs, log_q=log_q, weights=weights, item_owner=item_owner, item_row=item_row)


def reference(queries, item_vecs, log_q, weights, item_owner, item_row):
    width = queries.shape[1]
    per_item = B_DEV + M_DEV
    norm = BATCH / jnp.sum(weights.astype(jnp.float32))
    query_blocks = queries.reshape(N_GRP, N_DP, B_DEV, width)
    item_blocks = item_vecs.reshape(N_GRP, N_DP, per_item, width)
    bias_blocks = log_q.astype(jnp.float32).reshape(N_GRP, N_DP, per_item)
    weight_blocks = weights.astype(jnp.float32).reshape(N_GRP, N_DP, B_DEV)
    example = jnp.arange(N_GRP * B_DEV, dtype=jnp.int32)
    target = (example // B_DEV) * per_item + example % B_DEV
    columns = jnp.arange(N_GRP * per_item, dtype=jnp.int32)
    positive = (columns[None, :] == target[:, None]).astype(jnp.float32)

    def one_group(index):
        group_queries = lax.dynamic_index_in_dim(query_blocks, index, 1, keepdims=False).reshape(N_GRP * B_DEV, width)
        candidates = lax.dynamic_index_in_dim(item_blocks, index, 1, keepdims=False).reshape(N_GRP * per_item, width)
        item_bias = lax.dynamic_index_in_dim(bias_blocks, index, 1, keepdims=False).reshape(N_GRP * per_item)
        group_weights = lax.dynamic_index_in_dim(weight_blocks, index, 1, keepdims=False).reshape(N_GRP * B_DEV)
        logits = jnp.dot(group_queries, candidates.T, preferred_element_type=jnp.float32) - item_bias[None, :]
        shares = jax.nn.softmax(logits, axis=1)
        logit_grad = ((group_weights * norm)[:, None] * (shares - positive)).astype(jnp.bfloat16)
        query_part = jnp.dot(logit_grad, candidates, preferred_element_type=jnp.float32).astype(jnp.bfloat16)
        item_part = jnp.dot(logit_grad.T, group_queries, preferred_element_type=jnp.float32).astype(jnp.bfloat16)
        return query_part, item_part

    query_parts, item_parts = lax.map(one_group, jnp.arange(N_DP, dtype=jnp.int32))
    query_grad = query_parts.reshape(N_DP, N_GRP, B_DEV, width).transpose(1, 0, 2, 3).reshape(BATCH, width)
    item_grad = item_parts.reshape(N_DP, N_GRP, per_item, width).transpose(1, 0, 2, 3).reshape(ITEMS, width)
    block = jnp.arange(ITEMS, dtype=jnp.int32) // per_item
    dest = ((block // N_DP) * N_DP + item_owner[:, 0].astype(jnp.int32)) * ROWS_DEV + item_row.astype(jnp.int32)
    table_grad = jnp.zeros((TABLE_ROWS, width), jnp.float32).at[dest].add(item_grad.astype(jnp.float32))
    return query_grad, table_grad
```

```python
import functools

import jax
import jax.numpy as jnp
from jax import lax
from jax.experimental import pallas as pl
from jax.experimental.pallas import tpu as pltpu
from jax.sharding import PartitionSpec as P

N_X = 4
N_GRP = 8
N_Z = 12
N_Y = 8
B_DEV = 128
PER_ITEM = 160
PAD_ITEM = 176
ROWS_DEV = 1024
D = 256
BATCH = 98304
MESH = pl.DeviceIdType.MESH
HIGHEST = lax.Precision.HIGHEST


def nt_dot(left, right, precision=None):
    return lax.dot_general(
        left, right, (((1,), (1,)), ((), ())), precision=precision, preferred_element_type=jnp.float32
    )


def tn_dot(left, right):
    return lax.dot_general(left, right, (((0,), (0,)), ((), ())), preferred_element_type=jnp.float32)


def iota(shape, dim):
    return lax.broadcasted_iota(jnp.int32, shape, dim)


def kernel(
    q_ref, it_ref, lq_ref, w_ref, own_ref, row_ref,
    dq_ref, tab_ref,
    items_all, q_all, logits, probs, cross, grads, stats,
    ids1_send, ids1_recv, ids1_flat, ids2_send, ids2_recv,
    slots, perm, member, send1, recv1, send2, recv2,
    it_send_sem, it_recv_sem, q_send_sem, q_recv_sem, st_send_sem, st_recv_sem,
    i1_send_sem, i1_recv_sem, i2_send_sem, i2_recv_sem,
    r1_send_sem, r1_recv_sem, r2_send_sem, r2_recv_sem,
):
    g = lax.axis_index("grp")
    d = lax.axis_index("dp")
    z, y = d // N_Y, d % N_Y
    x, c = g // 2, g % 2
    sib = 2 * x + 1 - c
    ahead = 1 - 2 * c

    barrier = pltpu.get_barrier_semaphore()

    def greet_grp(j, carry):
        pl.semaphore_signal(barrier, inc=1, device_id={"grp": (g + j) % N_GRP}, device_id_type=MESH)
        return carry

    def greet_z(j, carry):
        pl.semaphore_signal(barrier, inc=1, device_id={"dp": ((z + j) % N_Z) * N_Y + y}, device_id_type=MESH)
        return carry

    def greet_y(j, carry):
        pl.semaphore_signal(barrier, inc=1, device_id={"dp": z * N_Y + (y + j) % N_Y}, device_id_type=MESH)
        return carry

    lax.fori_loop(1, N_GRP, greet_grp, 0)
    lax.fori_loop(1, N_Z, greet_z, 0)
    lax.fori_loop(1, N_Y, greet_y, 0)

    log_q = lq_ref[...].astype(jnp.float32)
    weights = w_ref[...].astype(jnp.float32)
    owner_i = own_ref[...]
    row_i = row_ref[...]
    items_all[g, 0:PER_ITEM, :] = it_ref[...]
    padded_lq = jnp.concatenate([log_q, jnp.zeros((1, D - PER_ITEM), jnp.float32)], axis=1)
    items_all[g, PER_ITEM:PAD_ITEM, :] = jnp.broadcast_to(padded_lq, (16, D)).astype(jnp.bfloat16)
    q_all[g] = q_ref[...]

    owner = owner_i.astype(jnp.float32)
    sub, lane = iota((PER_ITEM, PER_ITEM), 0), iota((PER_ITEM, PER_ITEM), 1)
    eye = sub == lane
    owner_col = jnp.sum(jnp.where(eye, owner, 0.0), axis=1, keepdims=True)
    lq_col = jnp.sum(jnp.where(eye, log_q, 0.0), axis=1, keepdims=True)
    same = jnp.where((owner_col == owner) & (sub < lane), 1.0, 0.0)
    place = jnp.sum(same, axis=0, keepdims=True).astype(jnp.int32)
    dest_z = owner_i // N_Y
    slot = owner_i * 2 + place
    slot_z = slot - dest_z * (2 * N_Y)

    kind = iota((48, PER_ITEM), 0) // 16
    sub48 = iota((48, PER_ITEM), 0) % 16
    part = jnp.where(kind == 0, row_i // 32, jnp.where(kind == 1, row_i % 32, 1)).astype(jnp.float32)
    left = jnp.where(sub48 == dest_z, part, 0.0).astype(jnp.bfloat16)
    right = jnp.where(iota((128, PER_ITEM), 0) == slot_z, 1.0, 0.0).astype(jnp.bfloat16)
    found = nt_dot(left, right)
    ids1 = found[0:16] * 32.0 + found[16:32] + found[32:48]
    ids1 = jnp.where(iota((16, 128), 1) == 2 * N_Y, jnp.sum(weights, axis=1, keepdims=True), ids1)
    for k in range(N_Z):
        ids1_send[k] = ids1[k : k + 1]
    ids1_recv[z] = ids1_send[z]

    pl.semaphore_wait(barrier, (N_GRP - 1) + (N_Z - 1) + (N_Y - 1))

    def block_copy(buf, block, target, send_sem, recv_sem, index):
        return pltpu.make_async_remote_copy(
            src_ref=buf.at[block],
            dst_ref=buf.at[block],
            send_sem=send_sem.at[index],
            recv_sem=recv_sem.at[block],
            device_id={"grp": target},
            device_id_type=MESH,
        )

    def chip(dx):
        return (x + dx + N_X) % N_X

    behind_x, ahead_x, far_x = chip(-ahead), chip(ahead), chip(2)
    behind_g, ahead_g, far_g = 2 * behind_x + c, 2 * ahead_x + c, 2 * far_x + c
    sent = []

    def send(buf, block, target, sems, index):
        copy = block_copy(buf, block, target, sems[0], sems[1], index)
        copy.start()
        sent.append(copy)

    def arrived(buf, block, sems):
        block_copy(buf, block, sib, sems[0], sems[1], 0).wait_recv()

    it_sems = (it_send_sem, it_recv_sem)
    q_sems = (q_send_sem, q_recv_sem)

    def first_sends(buf, sems):
        send(buf, g, ahead_g, sems, 0)
        send(buf, g, behind_g, sems, 1)
        send(buf, g, sib, sems, 2)

    first_sends(items_all, it_sems)

    def ids1_copy(j):
        zt = (z + j) % N_Z
        return pltpu.make_async_remote_copy(
            src_ref=ids1_send.at[zt],
            dst_ref=ids1_recv.at[z],
            send_sem=i1_send_sem,
            recv_sem=i1_recv_sem,
            device_id={"dp": zt * N_Y + y},
            device_id_type=MESH,
        )

    def start_ids1(j, carry):
        ids1_copy(j).start()
        return carry

    lax.fori_loop(1, N_Z, start_ids1, 0)
    first_sends(q_all, q_sems)

    slots[...] = jnp.where(iota((2 * N_Z * N_Y, PER_ITEM), 0) == slot, 1.0, 0.0).astype(jnp.bfloat16)
    pr, pc = iota((N_Y * 32, 2 * N_Z * N_Y), 0), iota((N_Y * 32, 2 * N_Z * N_Y), 1)
    in_y = pr % 32
    perm[...] = jnp.where(
        (in_y < 2 * N_Z) & (pc == (in_y // 2) * (2 * N_Y) + (pr // 32) * 2 + in_y % 2), 1.0, 0.0
    ).astype(jnp.bfloat16)

    ones = jnp.ones((B_DEV, D), jnp.bfloat16)
    diag = iota((PER_ITEM, D), 0) == iota((PER_ITEM, D), 1)

    def block_logits(block, top):
        lq = items_all[block, PER_ITEM:PAD_ITEM, :].astype(jnp.float32)[0:1]
        bias = jnp.where(diag, lq, 0.0).astype(jnp.bfloat16)
        value = nt_dot(items_all[block, 0:PER_ITEM, :], q_ref[...]) - nt_dot(bias, ones)
        logits[block] = value
        here = jnp.max(value, axis=0, keepdims=True)
        return here if top is None else jnp.maximum(top, here)

    def block_cross(block):
        cross[block] = nt_dot(it_ref[...], q_all[block]) - lq_col

    top = block_logits(g, None)
    block_cross(g)

    arrived(items_all, behind_g, it_sems)
    send(items_all, behind_g, ahead_g, it_sems, 3)
    send(items_all, behind_g, sib, it_sems, 4)
    arrived(items_all, ahead_g, it_sems)
    send(items_all, ahead_g, sib, it_sems, 5)
    top = block_logits(behind_g, top)
    top = block_logits(ahead_g, top)

    pltpu.make_async_copy(ids1_recv.at[pl.ds(0, N_Z - 1)], ids1_recv.at[pl.ds(0, N_Z - 1)], i1_recv_sem).wait()
    ids1_flat[...] = jnp.zeros((16, 128), jnp.float32)
    for k in range(N_Z):
        ids1_flat[k : k + 1, :] = ids1_recv[k]
    got1 = ids1_flat[...]
    y_sub, l_lane = iota((N_Y, 128), 0), iota((N_Y, 128), 1)
    z_sub, s_lane = iota((16, D), 0), iota((16, D), 1)
    ids2 = jnp.zeros((N_Y, D), jnp.float32)
    for k in range(2):
        pick = jnp.where(l_lane == 2 * y_sub + k, 1.0, 0.0)
        spread = jnp.where(s_lane == y * 32 + 2 * z_sub + k, 1.0, 0.0)
        picked = nt_dot(pick, got1, HIGHEST)
        ids2 = ids2 + jnp.dot(picked, spread, precision=HIGHEST, preferred_element_type=jnp.float32)
    summed = jnp.sum(got1, axis=0, keepdims=True)
    w_z = jnp.sum(jnp.where(iota((1, 128), 1) == 2 * N_Y, summed, 0.0), axis=1, keepdims=True)
    ids2 = jnp.where(iota((N_Y, D), 1) == y * 32 + 24, w_z, ids2)
    for k in range(N_Y):
        ids2_send[k] = ids2[k : k + 1]
    ids2_recv[y] = ids2_send[y]

    def ids2_copy(j):
        yt = (y + j) % N_Y
        return pltpu.make_async_remote_copy(
            src_ref=ids2_send.at[yt],
            dst_ref=ids2_recv.at[y],
            send_sem=i2_send_sem,
            recv_sem=i2_recv_sem,
            device_id={"dp": z * N_Y + yt},
            device_id_type=MESH,
        )

    def start_ids2(j, carry):
        ids2_copy(j).start()
        return carry

    lax.fori_loop(1, N_Y, start_ids2, 0)

    arrived(q_all, behind_g, q_sems)
    send(q_all, behind_g, ahead_g, q_sems, 3)
    send(q_all, behind_g, sib, q_sems, 4)
    arrived(q_all, ahead_g, q_sems)
    send(q_all, ahead_g, sib, q_sems, 5)
    arrived(items_all, far_g, it_sems)
    send(items_all, far_g, sib, it_sems, 6)
    top = block_logits(far_g, top)
    block_cross(behind_g)
    block_cross(ahead_g)
    for other in (x, behind_x, ahead_x, far_x):
        block = 2 * other + 1 - c
        arrived(items_all, block, it_sems)
        top = block_logits(block, top)
    arrived(q_all, far_g, q_sems)
    send(q_all, far_g, sib, q_sems, 6)

    total = jnp.zeros((1, B_DEV), jnp.float32)
    for b in range(N_GRP):
        shifted = jnp.exp(logits[b] - top)
        logits[b] = shifted
        total = total + jnp.sum(shifted, axis=0, keepdims=True)

    pltpu.make_async_copy(ids2_recv.at[pl.ds(0, N_Y - 1)], ids2_recv.at[pl.ds(0, N_Y - 1)], i2_recv_sem).wait()
    got2 = ids2_recv[0]
    for k in range(1, N_Y):
        got2 = got2 + ids2_recv[k]
    in_block = iota((1, D), 1) % 32
    slab = jnp.sum(jnp.where(in_block == 24, got2, 0.0), axis=1, keepdims=True)
    row_ids = jnp.where(in_block < 2 * N_Z, got2, 0.0).astype(jnp.int32)

    stats[g, :, 0:128] = top
    stats[g, :, 128:256] = 1.0 / total
    stats[g, :, 256:384] = weights
    stats[g, :, 384:512] = jnp.broadcast_to(slab, (1, 128))

    def stats_copy(j):
        return block_copy(stats, g, (g + j) % N_GRP, st_send_sem, st_recv_sem, j)

    def start_stats(j, carry):
        stats_copy(j).start()
        return carry

    lax.fori_loop(1, N_GRP, start_stats, 0)

    block_cross(far_g)
    for other in (x, behind_x, ahead_x, far_x):
        block = 2 * other + 1 - c
        arrived(q_all, block, q_sems)
        block_cross(block)

    def wait_stats(j, carry):
        block_copy(stats, (g + j) % N_GRP, sib, st_send_sem, st_recv_sem, 0).wait_recv()
        return carry

    lax.fori_loop(1, N_GRP, wait_stats, 0)

    weight_sum = stats[0, :, 384:512]
    for b in range(1, N_GRP):
        weight_sum = weight_sum + stats[b, :, 384:512]
    norm = BATCH / weight_sum
    pos_sub, pos_lane = iota((PER_ITEM, B_DEV), 0), iota((PER_ITEM, B_DEV), 1)
    for b in range(N_GRP):
        share = jnp.exp(cross[b] - stats[b, :, 0:128]) * stats[b, :, 128:256]
        share = share - jnp.where(pos_sub + b * PER_ITEM == pos_lane + g * PER_ITEM, 1.0, 0.0)
        grads[:, b * B_DEV : (b + 1) * B_DEV] = (stats[b, :, 256:384] * norm * share).astype(jnp.bfloat16)
    item_grad = jnp.dot(
        grads[...], q_all[...].reshape(N_GRP * B_DEV, D), preferred_element_type=jnp.float32
    ).astype(jnp.bfloat16)
    placed = jnp.dot(slots[...], item_grad, preferred_element_type=jnp.float32)
    send1[...] = placed.astype(jnp.bfloat16).reshape(N_Z, 2 * N_Y, D)

    def rows1_copy(j):
        zt = (z + j) % N_Z
        return pltpu.make_async_remote_copy(
            src_ref=send1.at[zt],
            dst_ref=recv1.at[z],
            send_sem=r1_send_sem,
            recv_sem=r1_recv_sem,
            device_id={"dp": zt * N_Y + y},
            device_id_type=MESH,
        )

    def start_rows1(j, carry):
        rows1_copy(j).start()
        return carry

    lax.fori_loop(1, N_Z, start_rows1, 0)
    recv1[z] = send1[z]

    member[...] = jnp.where(iota((ROWS_DEV, D), 0) + 1 == row_ids, 1.0, 0.0).astype(jnp.bfloat16)
    factor = weights * norm
    inverse = 1.0 / total
    for b in range(N_GRP):
        share = logits[b] * inverse
        share = share - jnp.where(pos_sub + b * PER_ITEM == pos_lane + g * PER_ITEM, 1.0, 0.0)
        probs[b, 0:PER_ITEM, :] = (factor * share).astype(jnp.bfloat16)
        probs[b, PER_ITEM:PAD_ITEM, :] = jnp.zeros((PAD_ITEM - PER_ITEM, B_DEV), jnp.bfloat16)
    dq_ref[...] = tn_dot(
        probs[...].reshape(N_GRP * PAD_ITEM, B_DEV), items_all[...].reshape(N_GRP * PAD_ITEM, D)
    ).astype(jnp.bfloat16)

    pltpu.make_async_copy(recv1.at[pl.ds(0, N_Z - 1)], recv1.at[pl.ds(0, N_Z - 1)], r1_recv_sem).wait()
    turned = jnp.dot(perm[...], recv1[...].reshape(2 * N_Z * N_Y, D), preferred_element_type=jnp.float32)
    send2[...] = turned.astype(jnp.bfloat16).reshape(N_Y, 32, D)

    def rows2_copy(j):
        yt = (y + j) % N_Y
        return pltpu.make_async_remote_copy(
            src_ref=send2.at[yt],
            dst_ref=recv2.at[y],
            send_sem=r2_send_sem,
            recv_sem=r2_recv_sem,
            device_id={"dp": z * N_Y + yt},
            device_id_type=MESH,
        )

    def start_rows2(j, carry):
        rows2_copy(j).start()
        return carry

    lax.fori_loop(1, N_Y, start_rows2, 0)
    recv2[y] = send2[y]

    for copy in sent:
        copy.wait_send()
    def wait_stats_sent(j, carry):
        stats_copy(j).wait_send()
        return carry

    lax.fori_loop(1, N_GRP, wait_stats_sent, 0)
    pltpu.make_async_copy(ids1_send.at[pl.ds(0, N_Z - 1)], ids1_send.at[pl.ds(0, N_Z - 1)], i1_send_sem).wait()
    pltpu.make_async_copy(ids2_send.at[pl.ds(0, N_Y - 1)], ids2_send.at[pl.ds(0, N_Y - 1)], i2_send_sem).wait()
    pltpu.make_async_copy(send1.at[pl.ds(0, N_Z - 1)], send1.at[pl.ds(0, N_Z - 1)], r1_send_sem).wait()
    pltpu.make_async_copy(recv2.at[pl.ds(0, N_Y - 1)], recv2.at[pl.ds(0, N_Y - 1)], r2_recv_sem).wait()
    tab_ref[...] = jnp.dot(member[...], recv2[...].reshape(N_Y * 32, D), preferred_element_type=jnp.float32)
    pltpu.make_async_copy(send2.at[pl.ds(0, N_Y - 1)], send2.at[pl.ds(0, N_Y - 1)], r2_send_sem).wait()


def shards(queries, item_vecs, log_q, weights, item_owner, item_row):
    vmem = pl.BlockSpec(memory_space=pltpu.VMEM)
    bf16, f32 = jnp.bfloat16, jnp.float32
    dma = pltpu.SemaphoreType.DMA
    return pl.pallas_call(
        kernel,
        out_shape=(
            jax.ShapeDtypeStruct((B_DEV, D), bf16),
            jax.ShapeDtypeStruct((ROWS_DEV, D), f32),
        ),
        in_specs=[vmem] * 6,
        out_specs=(vmem, vmem),
        scratch_shapes=[
            pltpu.VMEM((N_GRP, PAD_ITEM, D), bf16),
            pltpu.VMEM((N_GRP, B_DEV, D), bf16),
            pltpu.VMEM((N_GRP, PER_ITEM, B_DEV), f32),
            pltpu.VMEM((N_GRP, PAD_ITEM, B_DEV), bf16),
            pltpu.VMEM((N_GRP, PER_ITEM, B_DEV), f32),
            pltpu.VMEM((PER_ITEM, N_GRP * B_DEV), bf16),
            pltpu.VMEM((N_GRP, 1, 512), f32),
            pltpu.VMEM((N_Z, 1, 128), f32),
            pltpu.VMEM((N_Z, 1, 128), f32),
            pltpu.VMEM((16, 128), f32),
            pltpu.VMEM((N_Y, 1, D), f32),
            pltpu.VMEM((N_Y, 1, D), f32),
            pltpu.VMEM((2 * N_Z * N_Y, PER_ITEM), bf16),
            pltpu.VMEM((N_Y * 32, 2 * N_Z * N_Y), bf16),
            pltpu.VMEM((ROWS_DEV, D), bf16),
            pltpu.VMEM((N_Z, 2 * N_Y, D), bf16),
            pltpu.VMEM((N_Z, 2 * N_Y, D), bf16),
            pltpu.VMEM((N_Y, 32, D), bf16),
            pltpu.VMEM((N_Y, 32, D), bf16),
            dma((7,)), dma((N_GRP,)),
            dma((7,)), dma((N_GRP,)),
            dma((N_GRP,)), dma((N_GRP,)),
            dma, dma, dma, dma, dma, dma, dma, dma,
        ],
        compiler_params=pltpu.CompilerParams(
            collective_id=0, has_side_effects=True, vmem_limit_bytes=32 * 1024 * 1024
        ),
    )(
        queries,
        item_vecs,
        log_q.reshape(1, PER_ITEM),
        weights.reshape(1, B_DEV),
        item_owner.reshape(1, PER_ITEM),
        item_row.reshape(1, PER_ITEM),
    )


def solution(mesh):
    in_specs = (
        P(("grp", "dp"), None),
        P(("grp", "dp"), None),
        P(("grp", "dp")),
        P(("grp", "dp")),
        P(("grp", "dp"), None),
        P(("grp", "dp")),
    )
    out_specs = (P(("grp", "dp"), None), P(("grp", "dp"), None))
    return jax.shard_map(shards, mesh=mesh, in_specs=in_specs, out_specs=out_specs, check_vma=False)
```

```python
import functools

import jax
import jax.numpy as jnp
from jax import lax
from jax.experimental import pallas as pl
from jax.experimental.pallas import tpu as pltpu
from jax.sharding import PartitionSpec as P

N_X = 4
N_GRP = 8
N_Z = 12
N_Y = 8
B_DEV = 128
PER_ITEM = 160
PAD_ITEM = 176
ROWS_DEV = 1024
D = 256
BATCH = 98304
MESH = pl.DeviceIdType.MESH
HIGHEST = lax.Precision.HIGHEST


def nt_dot(left, right, precision=None):
    return lax.dot_general(
        left, right, (((1,), (1,)), ((), ())), precision=precision, preferred_element_type=jnp.float32
    )


def tn_dot(left, right):
    return lax.dot_general(left, right, (((0,), (0,)), ((), ())), preferred_element_type=jnp.float32)


def iota(shape, dim):
    return lax.broadcasted_iota(jnp.int32, shape, dim)


def kernel(
    q_hbm, it_hbm, lq_hbm, w_hbm, own_hbm, row_hbm,
    dq_ref, tab_ref,
    lq_ref, w_ref, own_ref, row_ref, slabs,
    items_all, q_all, logits, probs, cross, grads, stats,
    ids1_send, ids1_recv, ids1_flat, ids2_send, ids2_recv,
    slots, perm, member, send1, recv1, send2, recv2,
    in_sem, sl_send_sem, sl_recv_sem,
    it_send_sem, it_recv_sem, q_send_sem, q_recv_sem, st_send_sem, st_recv_sem,
    i1_send_sem, i1_recv_sem, i2_send_sem, i2_recv_sem,
    r1_send_sem, r1_recv_sem, r2_send_sem, r2_recv_sem,
):
    g = lax.axis_index("grp")
    d = lax.axis_index("dp")
    z, y = d // N_Y, d % N_Y
    x, c = g // 2, g % 2
    sib = 2 * x + 1 - c
    ahead = 1 - 2 * c

    loads = [
        pltpu.make_async_copy(src, dst, in_sem.at[i])
        for i, (src, dst) in enumerate((
            (it_hbm, items_all.at[g, pl.ds(0, PER_ITEM)]),
            (q_hbm, q_all.at[g]),
            (lq_hbm, lq_ref),
            (w_hbm, w_ref),
            (own_hbm, own_ref),
            (row_hbm, row_ref),
        ))
    ]
    for load in loads:
        load.start()

    barrier = pltpu.get_barrier_semaphore()

    def greet_grp(j, carry):
        pl.semaphore_signal(barrier, inc=1, device_id={"grp": (g + j) % N_GRP}, device_id_type=MESH)
        return carry

    def greet_z(j, carry):
        pl.semaphore_signal(barrier, inc=1, device_id={"dp": ((z + j) % N_Z) * N_Y + y}, device_id_type=MESH)
        return carry

    def greet_y(j, carry):
        pl.semaphore_signal(barrier, inc=1, device_id={"dp": z * N_Y + (y + j) % N_Y}, device_id_type=MESH)
        return carry

    lax.fori_loop(1, N_GRP, greet_grp, 0)
    lax.fori_loop(1, N_Z, greet_z, 0)
    lax.fori_loop(1, N_Y, greet_y, 0)

    for load in loads:
        load.wait()
    log_q = lq_ref[...].astype(jnp.float32).reshape(1, PER_ITEM)
    padded_lq = jnp.concatenate([log_q, jnp.zeros((1, D - PER_ITEM), jnp.float32)], axis=1)
    items_all[g, PER_ITEM:PAD_ITEM, :] = jnp.broadcast_to(padded_lq, (16, D)).astype(jnp.bfloat16)

    pl.semaphore_wait(barrier, (N_GRP - 1) + (N_Z - 1) + (N_Y - 1))

    def block_copy(buf, block, target, send_sem, recv_sem, index):
        return pltpu.make_async_remote_copy(
            src_ref=buf.at[block],
            dst_ref=buf.at[block],
            send_sem=send_sem.at[index],
            recv_sem=recv_sem.at[block],
            device_id={"grp": target},
            device_id_type=MESH,
        )

    def chip(dx):
        return (x + dx + N_X) % N_X

    behind_x, ahead_x, far_x = chip(-ahead), chip(ahead), chip(2)
    behind_g, ahead_g, far_g = 2 * behind_x + c, 2 * ahead_x + c, 2 * far_x + c
    sent = []

    def send(buf, block, target, sems, index):
        copy = block_copy(buf, block, target, sems[0], sems[1], index)
        copy.start()
        sent.append(copy)

    def arrived(buf, block, sems):
        block_copy(buf, block, sib, sems[0], sems[1], 0).wait_recv()

    it_sems = (it_send_sem, it_recv_sem)
    q_sems = (q_send_sem, q_recv_sem)

    def first_sends(buf, sems):
        send(buf, g, ahead_g, sems, 0)
        send(buf, g, behind_g, sems, 1)
        send(buf, g, sib, sems, 2)

    first_sends(items_all, it_sems)
    first_sends(q_all, q_sems)

    weights = w_ref[...].astype(jnp.float32).reshape(1, B_DEV)
    owner_i = own_ref[...]
    row_i = row_ref[...]

    owner = owner_i.astype(jnp.float32)
    sub, lane = iota((PER_ITEM, PER_ITEM), 0), iota((PER_ITEM, PER_ITEM), 1)
    eye = sub == lane
    owner_col = jnp.sum(jnp.where(eye, owner, 0.0), axis=1, keepdims=True)
    lq_col = jnp.sum(jnp.where(eye, log_q, 0.0), axis=1, keepdims=True)
    same = jnp.where((owner_col == owner) & (sub < lane), 1.0, 0.0)
    place = jnp.sum(same, axis=0, keepdims=True).astype(jnp.int32)
    dest_z = owner_i // N_Y
    slot = owner_i * 2 + place
    slot_z = slot - dest_z * (2 * N_Y)

    kind = iota((48, PER_ITEM), 0) // 16
    sub48 = iota((48, PER_ITEM), 0) % 16
    part = jnp.where(kind == 0, row_i // 32, jnp.where(kind == 1, row_i % 32, 1)).astype(jnp.float32)
    left = jnp.where(sub48 == dest_z, part, 0.0).astype(jnp.bfloat16)
    right = jnp.where(iota((128, PER_ITEM), 0) == slot_z, 1.0, 0.0).astype(jnp.bfloat16)
    found = nt_dot(left, right)
    ids1 = found[0:16] * 32.0 + found[16:32] + found[32:48]
    ids1 = jnp.where(iota((16, 128), 1) == 2 * N_Y, jnp.sum(weights, axis=1, keepdims=True), ids1)
    for k in range(N_Z):
        ids1_send[k] = ids1[k : k + 1]
    ids1_recv[z] = ids1_send[z]


    def ids1_copy(j):
        zt = (z + j) % N_Z
        return pltpu.make_async_remote_copy(
            src_ref=ids1_send.at[zt],
            dst_ref=ids1_recv.at[z],
            send_sem=i1_send_sem,
            recv_sem=i1_recv_sem,
            device_id={"dp": zt * N_Y + y},
            device_id_type=MESH,
        )

    def start_ids1(j, carry):
        ids1_copy(j).start()
        return carry

    lax.fori_loop(1, N_Z, start_ids1, 0)

    slots[...] = jnp.where(iota((2 * N_Z * N_Y, PER_ITEM), 0) == slot, 1.0, 0.0).astype(jnp.bfloat16)
    pr, pc = iota((N_Y * 32, 2 * N_Z * N_Y), 0), iota((N_Y * 32, 2 * N_Z * N_Y), 1)
    in_y = pr % 32
    perm[...] = jnp.where(
        (in_y < 2 * N_Z) & (pc == (in_y // 2) * (2 * N_Y) + (pr // 32) * 2 + in_y % 2), 1.0, 0.0
    ).astype(jnp.bfloat16)

    ones = jnp.ones((B_DEV, D), jnp.bfloat16)
    diag = iota((PER_ITEM, D), 0) == iota((PER_ITEM, D), 1)

    def block_logits(block, top):
        lq = items_all[block, PER_ITEM:PAD_ITEM, :].astype(jnp.float32)[0:1]
        bias = jnp.where(diag, lq, 0.0).astype(jnp.bfloat16)
        value = nt_dot(items_all[block, 0:PER_ITEM, :], q_all[g]) - nt_dot(bias, ones)
        logits[block] = value
        here = jnp.max(value, axis=0, keepdims=True)
        return here if top is None else jnp.maximum(top, here)

    def block_cross(block):
        cross[block] = nt_dot(items_all[g, 0:PER_ITEM, :], q_all[block]) - lq_col

    top = block_logits(g, None)
    block_cross(g)

    arrived(items_all, behind_g, it_sems)
    send(items_all, behind_g, ahead_g, it_sems, 3)
    send(items_all, behind_g, sib, it_sems, 4)
    arrived(items_all, ahead_g, it_sems)
    send(items_all, ahead_g, sib, it_sems, 5)
    arrived(q_all, behind_g, q_sems)
    send(q_all, behind_g, ahead_g, q_sems, 3)
    send(q_all, behind_g, sib, q_sems, 4)
    arrived(q_all, ahead_g, q_sems)
    send(q_all, ahead_g, sib, q_sems, 5)
    top = block_logits(behind_g, top)
    top = block_logits(ahead_g, top)
    arrived(items_all, far_g, it_sems)
    send(items_all, far_g, sib, it_sems, 6)
    top = block_logits(far_g, top)
    arrived(q_all, far_g, q_sems)
    send(q_all, far_g, sib, q_sems, 6)
    for other in (x, behind_x, ahead_x, far_x):
        block = 2 * other + 1 - c
        arrived(items_all, block, it_sems)
        top = block_logits(block, top)

    total = jnp.zeros((1, B_DEV), jnp.float32)
    for b in range(N_GRP):
        shifted = jnp.exp(logits[b] - top)
        logits[b] = shifted
        total = total + jnp.sum(shifted, axis=0, keepdims=True)

    stats[g, :, 0:128] = top
    stats[g, :, 128:256] = 1.0 / total
    stats[g, :, 256:384] = weights

    def stats_copy(j):
        return block_copy(stats, g, (g + j) % N_GRP, st_send_sem, st_recv_sem, j)

    def start_stats(j, carry):
        stats_copy(j).start()
        return carry

    lax.fori_loop(1, N_GRP, start_stats, 0)

    pltpu.make_async_copy(ids1_recv.at[pl.ds(0, N_Z - 1)], ids1_recv.at[pl.ds(0, N_Z - 1)], i1_recv_sem).wait()
    ids1_flat[...] = jnp.zeros((16, 128), jnp.float32)
    for k in range(N_Z):
        ids1_flat[k : k + 1, :] = ids1_recv[k]
    got1 = ids1_flat[...]
    y_sub, l_lane = iota((N_Y, 128), 0), iota((N_Y, 128), 1)
    z_sub, s_lane = iota((16, D), 0), iota((16, D), 1)
    ids2 = jnp.zeros((N_Y, D), jnp.float32)
    for k in range(2):
        pick = jnp.where(l_lane == 2 * y_sub + k, 1.0, 0.0)
        spread = jnp.where(s_lane == y * 32 + 2 * z_sub + k, 1.0, 0.0)
        picked = nt_dot(pick, got1, HIGHEST)
        ids2 = ids2 + jnp.dot(picked, spread, precision=HIGHEST, preferred_element_type=jnp.float32)
    summed = jnp.sum(got1, axis=0, keepdims=True)
    w_z = jnp.sum(jnp.where(iota((1, 128), 1) == 2 * N_Y, summed, 0.0), axis=1, keepdims=True)
    ids2 = jnp.where(iota((N_Y, D), 1) == y * 32 + 24, w_z, ids2)
    for k in range(N_Y):
        ids2_send[k] = ids2[k : k + 1]
    ids2_recv[y] = ids2_send[y]

    def ids2_copy(j):
        yt = (y + j) % N_Y
        return pltpu.make_async_remote_copy(
            src_ref=ids2_send.at[yt],
            dst_ref=ids2_recv.at[y],
            send_sem=i2_send_sem,
            recv_sem=i2_recv_sem,
            device_id={"dp": z * N_Y + yt},
            device_id_type=MESH,
        )

    def start_ids2(j, carry):
        ids2_copy(j).start()
        return carry

    lax.fori_loop(1, N_Y, start_ids2, 0)

    block_cross(behind_g)
    block_cross(ahead_g)
    block_cross(far_g)
    for other in (x, behind_x, ahead_x, far_x):
        block = 2 * other + 1 - c
        arrived(q_all, block, q_sems)
        block_cross(block)

    def wait_stats(j, carry):
        block_copy(stats, (g + j) % N_GRP, sib, st_send_sem, st_recv_sem, 0).wait_recv()
        return carry

    lax.fori_loop(1, N_GRP, wait_stats, 0)

    pos_sub, pos_lane = iota((PER_ITEM, B_DEV), 0), iota((PER_ITEM, B_DEV), 1)
    for b in range(N_GRP):
        share = jnp.exp(cross[b] - stats[b, :, 0:128]) * stats[b, :, 128:256]
        share = share - jnp.where(pos_sub + b * PER_ITEM == pos_lane + g * PER_ITEM, 1.0, 0.0)
        grads[:, b * B_DEV : (b + 1) * B_DEV] = (stats[b, :, 256:384] * share).astype(jnp.bfloat16)
    item_grad = jnp.dot(
        grads[...], q_all[...].reshape(N_GRP * B_DEV, D), preferred_element_type=jnp.float32
    ).astype(jnp.bfloat16)
    placed = jnp.dot(slots[...], item_grad, preferred_element_type=jnp.float32)
    send1[...] = placed.astype(jnp.bfloat16).reshape(N_Z, 2 * N_Y, D)

    def rows1_copy(j):
        zt = (z + j) % N_Z
        return pltpu.make_async_remote_copy(
            src_ref=send1.at[zt],
            dst_ref=recv1.at[z],
            send_sem=r1_send_sem,
            recv_sem=r1_recv_sem,
            device_id={"dp": zt * N_Y + y},
            device_id_type=MESH,
        )

    def start_rows1(j, carry):
        rows1_copy(j).start()
        return carry

    lax.fori_loop(1, N_Z, start_rows1, 0)
    recv1[z] = send1[z]

    pltpu.make_async_copy(ids2_recv.at[pl.ds(0, N_Y - 1)], ids2_recv.at[pl.ds(0, N_Y - 1)], i2_recv_sem).wait()
    got2 = ids2_recv[0]
    for k in range(1, N_Y):
        got2 = got2 + ids2_recv[k]
    in_block = iota((1, D), 1) % 32
    slab = jnp.sum(jnp.where(in_block == 24, got2, 0.0), axis=1, keepdims=True)
    row_ids = jnp.where(in_block < 2 * N_Z, got2, 0.0).astype(jnp.int32)

    slabs[g] = jnp.broadcast_to(slab, (1, 128))

    def slab_copy(j):
        return block_copy(slabs, g, (g + j) % N_GRP, sl_send_sem, sl_recv_sem, j)

    def start_slabs(j, carry):
        slab_copy(j).start()
        return carry

    lax.fori_loop(1, N_GRP, start_slabs, 0)

    member[...] = jnp.where(iota((ROWS_DEV, D), 0) + 1 == row_ids, 1.0, 0.0).astype(jnp.bfloat16)
    inverse = 1.0 / total
    for b in range(N_GRP):
        share = logits[b] * inverse
        share = share - jnp.where(pos_sub + b * PER_ITEM == pos_lane + g * PER_ITEM, 1.0, 0.0)
        probs[b, 0:PER_ITEM, :] = (weights * share).astype(jnp.bfloat16)
        probs[b, PER_ITEM:PAD_ITEM, :] = jnp.zeros((PAD_ITEM - PER_ITEM, B_DEV), jnp.bfloat16)
    query_grad = tn_dot(
        probs[...].reshape(N_GRP * PAD_ITEM, B_DEV), items_all[...].reshape(N_GRP * PAD_ITEM, D)
    )

    def wait_slabs(j, carry):
        block_copy(slabs, (g + j) % N_GRP, sib, sl_send_sem, sl_recv_sem, 0).wait_recv()
        return carry

    lax.fori_loop(1, N_GRP, wait_slabs, 0)
    weight_sum = slabs[0]
    for b in range(1, N_GRP):
        weight_sum = weight_sum + slabs[b]
    norm = BATCH / weight_sum[:, 0:1]
    dq_ref[...] = (query_grad * norm).astype(jnp.bfloat16)

    pltpu.make_async_copy(recv1.at[pl.ds(0, N_Z - 1)], recv1.at[pl.ds(0, N_Z - 1)], r1_recv_sem).wait()
    turned = jnp.dot(perm[...], recv1[...].reshape(2 * N_Z * N_Y, D), preferred_element_type=jnp.float32)
    send2[...] = turned.astype(jnp.bfloat16).reshape(N_Y, 32, D)

    def rows2_copy(j):
        yt = (y + j) % N_Y
        return pltpu.make_async_remote_copy(
            src_ref=send2.at[yt],
            dst_ref=recv2.at[y],
            send_sem=r2_send_sem,
            recv_sem=r2_recv_sem,
            device_id={"dp": z * N_Y + yt},
            device_id_type=MESH,
        )

    def start_rows2(j, carry):
        rows2_copy(j).start()
        return carry

    lax.fori_loop(1, N_Y, start_rows2, 0)
    recv2[y] = send2[y]

    for copy in sent:
        copy.wait_send()
    def wait_stats_sent(j, carry):
        stats_copy(j).wait_send()
        slab_copy(j).wait_send()
        return carry

    lax.fori_loop(1, N_GRP, wait_stats_sent, 0)
    pltpu.make_async_copy(ids1_send.at[pl.ds(0, N_Z - 1)], ids1_send.at[pl.ds(0, N_Z - 1)], i1_send_sem).wait()
    pltpu.make_async_copy(ids2_send.at[pl.ds(0, N_Y - 1)], ids2_send.at[pl.ds(0, N_Y - 1)], i2_send_sem).wait()
    pltpu.make_async_copy(send1.at[pl.ds(0, N_Z - 1)], send1.at[pl.ds(0, N_Z - 1)], r1_send_sem).wait()
    pltpu.make_async_copy(recv2.at[pl.ds(0, N_Y - 1)], recv2.at[pl.ds(0, N_Y - 1)], r2_recv_sem).wait()
    tab_ref[...] = norm * jnp.dot(
        member[...], recv2[...].reshape(N_Y * 32, D), preferred_element_type=jnp.float32
    )
    pltpu.make_async_copy(send2.at[pl.ds(0, N_Y - 1)], send2.at[pl.ds(0, N_Y - 1)], r2_send_sem).wait()


def shards(queries, item_vecs, log_q, weights, item_owner, item_row):
    vmem = pl.BlockSpec(memory_space=pltpu.VMEM)
    bf16, f32 = jnp.bfloat16, jnp.float32
    dma = pltpu.SemaphoreType.DMA
    return pl.pallas_call(
        kernel,
        out_shape=(
            jax.ShapeDtypeStruct((B_DEV, D), bf16),
            jax.ShapeDtypeStruct((ROWS_DEV, D), f32),
        ),
        in_specs=[pl.BlockSpec(memory_space=pltpu.HBM)] * 6,
        out_specs=(vmem, vmem),
        scratch_shapes=[
            pltpu.VMEM((PER_ITEM,), bf16),
            pltpu.VMEM((B_DEV,), bf16),
            pltpu.VMEM((1, PER_ITEM), jnp.int32),
            pltpu.VMEM((1, PER_ITEM), jnp.int32),
            pltpu.VMEM((N_GRP, 1, 128), f32),
            pltpu.VMEM((N_GRP, PAD_ITEM, D), bf16),
            pltpu.VMEM((N_GRP, B_DEV, D), bf16),
            pltpu.VMEM((N_GRP, PER_ITEM, B_DEV), f32),
            pltpu.VMEM((N_GRP, PAD_ITEM, B_DEV), bf16),
            pltpu.VMEM((N_GRP, PER_ITEM, B_DEV), f32),
            pltpu.VMEM((PER_ITEM, N_GRP * B_DEV), bf16),
            pltpu.VMEM((N_GRP, 1, 384), f32),
            pltpu.VMEM((N_Z, 1, 128), f32),
            pltpu.VMEM((N_Z, 1, 128), f32),
            pltpu.VMEM((16, 128), f32),
            pltpu.VMEM((N_Y, 1, D), f32),
            pltpu.VMEM((N_Y, 1, D), f32),
            pltpu.VMEM((2 * N_Z * N_Y, PER_ITEM), bf16),
            pltpu.VMEM((N_Y * 32, 2 * N_Z * N_Y), bf16),
            pltpu.VMEM((ROWS_DEV, D), bf16),
            pltpu.VMEM((N_Z, 2 * N_Y, D), bf16),
            pltpu.VMEM((N_Z, 2 * N_Y, D), bf16),
            pltpu.VMEM((N_Y, 32, D), bf16),
            pltpu.VMEM((N_Y, 32, D), bf16),
            dma((6,)), dma((N_GRP,)), dma((N_GRP,)),
            dma((7,)), dma((N_GRP,)),
            dma((7,)), dma((N_GRP,)),
            dma((N_GRP,)), dma((N_GRP,)),
            dma, dma, dma, dma, dma, dma, dma, dma,
        ],
        compiler_params=pltpu.CompilerParams(
            collective_id=0, has_side_effects=True, vmem_limit_bytes=32 * 1024 * 1024
        ),
    )(*(
        pltpu.with_memory_space_constraint(operand, pltpu.HBM)
        for operand in (
            queries,
            item_vecs,
            log_q,
            weights,
            item_owner.reshape(1, PER_ITEM),
            item_row.reshape(1, PER_ITEM),
        )
    ))


def solution(mesh):
    in_specs = (
        P(("grp", "dp"), None),
        P(("grp", "dp"), None),
        P(("grp", "dp")),
        P(("grp", "dp")),
        P(("grp", "dp"), None),
        P(("grp", "dp")),
    )
    out_specs = (P(("grp", "dp"), None), P(("grp", "dp"), None))
    return jax.shard_map(shards, mesh=mesh, in_specs=in_specs, out_specs=out_specs, check_vma=False)
```

```python
import functools

import jax
import jax.numpy as jnp
from jax import lax
from jax.experimental import pallas as pl
from jax.experimental.pallas import tpu as pltpu
from jax.sharding import PartitionSpec as P

N_X = 4
N_GRP = 8
N_Z = 12
N_Y = 8
B_DEV = 128
PER_ITEM = 160
PAD_ITEM = 176
ROWS_DEV = 1024
D = 256
BATCH = 98304
MESH = pl.DeviceIdType.MESH
HIGHEST = lax.Precision.HIGHEST


def nt_dot(left, right, precision=None):
    return lax.dot_general(
        left, right, (((1,), (1,)), ((), ())), precision=precision, preferred_element_type=jnp.float32
    )


def tn_dot(left, right):
    return lax.dot_general(left, right, (((0,), (0,)), ((), ())), preferred_element_type=jnp.float32)


def iota(shape, dim):
    return lax.broadcasted_iota(jnp.int32, shape, dim)


def kernel(
    q_hbm, it_hbm, lq_hbm, w_hbm, own_hbm, row_hbm,
    dq_ref, tab_ref,
    lq_ref, w_ref, own_ref, row_ref,
    items_all, q_all, logits, probs, cross, grads, stats,
    ids1_send, ids1_recv, ids1_flat, ids2_send, ids2_recv,
    slots, perm, member, send1, recv1, send2, recv2,
    in_sem, z_sems, y_sems,
    it_send_sem, it_recv_sem, q_send_sem, q_recv_sem, st_send_sem, st_recv_sem,
    i1_send_sem, i1_recv_sem, i2_send_sem, i2_recv_sem,
    r1_send_sem, r1_recv_sem, r2_send_sem, r2_recv_sem,
):
    g = lax.axis_index("grp")
    d = lax.axis_index("dp")
    z, y = d // N_Y, d % N_Y
    x, c = g // 2, g % 2
    sib = 2 * x + 1 - c
    ahead = 1 - 2 * c

    loads = [
        pltpu.make_async_copy(src, dst, in_sem.at[i])
        for i, (src, dst) in enumerate((
            (it_hbm, items_all.at[g, pl.ds(0, PER_ITEM)]),
            (q_hbm, q_all.at[g]),
            (lq_hbm, lq_ref),
            (w_hbm, w_ref),
            (own_hbm, own_ref),
            (row_hbm, row_ref),
        ))
    ]
    for load in loads:
        load.start()

    barrier = pltpu.get_barrier_semaphore()

    def greet_grp(j, carry):
        pl.semaphore_signal(barrier, inc=1, device_id={"grp": (g + j) % N_GRP}, device_id_type=MESH)
        return carry

    lax.fori_loop(1, N_GRP, greet_grp, 0)

    def z_peer(step):
        return {"dp": ((z + step + N_Z) % N_Z) * N_Y + y}

    def y_peer(step):
        return {"dp": z * N_Y + (y + step + N_Y) % N_Y}

    def signal_pair(sem, peer, step):
        pl.semaphore_signal(sem, inc=1, device_id=peer(step), device_id_type=MESH)
        pl.semaphore_signal(sem, inc=1, device_id=peer(-step), device_id_type=MESH)

    signal_pair(barrier, z_peer, 1)
    signal_pair(barrier, y_peer, 1)

    for load in loads:
        load.wait()
    log_q = lq_ref[...].astype(jnp.float32).reshape(1, PER_ITEM)
    weights = w_ref[...].astype(jnp.float32).reshape(1, B_DEV)
    padded_lq = jnp.concatenate([log_q, jnp.zeros((1, D - PER_ITEM), jnp.float32)], axis=1)
    padded_w = jnp.concatenate([weights, jnp.zeros((1, D - B_DEV), jnp.float32)], axis=1)
    items_all[g, PER_ITEM:PAD_ITEM, :] = jnp.where(iota((16, D), 0) == 0, padded_lq, padded_w).astype(jnp.bfloat16)

    pl.semaphore_wait(barrier, (N_GRP - 1) + 2 + 2)

    def block_copy(buf, block, target, send_sem, recv_sem, index):
        return pltpu.make_async_remote_copy(
            src_ref=buf.at[block],
            dst_ref=buf.at[block],
            send_sem=send_sem.at[index],
            recv_sem=recv_sem.at[block],
            device_id={"grp": target},
            device_id_type=MESH,
        )

    def chip(dx):
        return (x + dx + N_X) % N_X

    behind_x, ahead_x, far_x = chip(-ahead), chip(ahead), chip(2)
    behind_g, ahead_g, far_g = 2 * behind_x + c, 2 * ahead_x + c, 2 * far_x + c
    sent = []

    def send(buf, block, target, sems, index):
        copy = block_copy(buf, block, target, sems[0], sems[1], index)
        copy.start()
        sent.append(copy)

    def arrived(buf, block, sems):
        block_copy(buf, block, sib, sems[0], sems[1], 0).wait_recv()

    it_sems = (it_send_sem, it_recv_sem)
    q_sems = (q_send_sem, q_recv_sem)

    def first_sends(buf, sems):
        send(buf, g, ahead_g, sems, 0)
        send(buf, g, behind_g, sems, 1)
        send(buf, g, sib, sems, 2)

    first_sends(items_all, it_sems)
    first_sends(q_all, q_sems)
    signal_pair(z_sems.at[0], z_peer, 1)
    signal_pair(y_sems.at[0], y_peer, 1)

    owner_i = own_ref[...]
    row_i = row_ref[...]

    owner = owner_i.astype(jnp.float32)
    sub, lane = iota((PER_ITEM, PER_ITEM), 0), iota((PER_ITEM, PER_ITEM), 1)
    eye = sub == lane
    owner_col = jnp.sum(jnp.where(eye, owner, 0.0), axis=1, keepdims=True)
    lq_col = jnp.sum(jnp.where(eye, log_q, 0.0), axis=1, keepdims=True)
    same = jnp.where((owner_col == owner) & (sub < lane), 1.0, 0.0)
    place = jnp.sum(same, axis=0, keepdims=True).astype(jnp.int32)
    dest_z = owner_i // N_Y
    slot = owner_i * 2 + place
    slot_z = slot - dest_z * (2 * N_Y)

    kind = iota((48, PER_ITEM), 0) // 16
    sub48 = iota((48, PER_ITEM), 0) % 16
    part = jnp.where(kind == 0, row_i // 32, jnp.where(kind == 1, row_i % 32, 1)).astype(jnp.float32)
    left = jnp.where(sub48 == dest_z, part, 0.0).astype(jnp.bfloat16)
    right = jnp.where(iota((128, PER_ITEM), 0) == slot_z, 1.0, 0.0).astype(jnp.bfloat16)
    found = nt_dot(left, right)
    ids1 = found[0:16] * 32.0 + found[16:32] + found[32:48]
    slots[...] = jnp.where(iota((2 * N_Z * N_Y, PER_ITEM), 0) == slot, 1.0, 0.0).astype(jnp.bfloat16)
    pr, pc = iota((N_Y * 32, 2 * N_Z * N_Y), 0), iota((N_Y * 32, 2 * N_Z * N_Y), 1)
    in_y = pr % 32
    perm[...] = jnp.where(
        (in_y < 2 * N_Z) & (pc == (in_y // 2) * (2 * N_Y) + (pr // 32) * 2 + in_y % 2), 1.0, 0.0
    ).astype(jnp.bfloat16)

    ones = jnp.ones((B_DEV, D), jnp.bfloat16)
    diag = iota((PER_ITEM, D), 0) == iota((PER_ITEM, D), 1)

    def block_logits(block, top):
        lq = items_all[block, PER_ITEM:PAD_ITEM, :].astype(jnp.float32)[0:1]
        bias = jnp.where(diag, lq, 0.0).astype(jnp.bfloat16)
        value = nt_dot(items_all[block, 0:PER_ITEM, :], q_all[g]) - nt_dot(bias, ones)
        logits[block] = value
        here = jnp.max(value, axis=0, keepdims=True)
        return here if top is None else jnp.maximum(top, here)

    def block_cross(block):
        cross[block] = nt_dot(items_all[g, 0:PER_ITEM, :], q_all[block]) - lq_col

    top = block_logits(g, None)
    block_cross(g)

    arrived(items_all, behind_g, it_sems)
    send(items_all, behind_g, ahead_g, it_sems, 3)
    send(items_all, behind_g, sib, it_sems, 4)
    arrived(items_all, ahead_g, it_sems)
    send(items_all, ahead_g, sib, it_sems, 5)
    pl.semaphore_wait(z_sems.at[0], 2)
    signal_pair(z_sems.at[1], z_peer, 2)
    pl.semaphore_wait(y_sems.at[0], 2)
    signal_pair(y_sems.at[1], y_peer, 2)
    arrived(q_all, behind_g, q_sems)
    send(q_all, behind_g, ahead_g, q_sems, 3)
    send(q_all, behind_g, sib, q_sems, 4)
    arrived(q_all, ahead_g, q_sems)
    send(q_all, ahead_g, sib, q_sems, 5)
    top = block_logits(behind_g, top)
    top = block_logits(ahead_g, top)
    arrived(items_all, far_g, it_sems)
    send(items_all, far_g, sib, it_sems, 6)
    top = block_logits(far_g, top)
    pl.semaphore_wait(z_sems.at[1], 2)
    signal_pair(z_sems.at[2], z_peer, 2)
    arrived(q_all, far_g, q_sems)
    send(q_all, far_g, sib, q_sems, 6)
    for other in (x, behind_x, ahead_x, far_x):
        block = 2 * other + 1 - c
        arrived(items_all, block, it_sems)
        top = block_logits(block, top)

    total = jnp.zeros((1, B_DEV), jnp.float32)
    for b in range(N_GRP):
        shifted = jnp.exp(logits[b] - top)
        logits[b] = shifted
        total = total + jnp.sum(shifted, axis=0, keepdims=True)

    stats[g, :, 0:128] = top
    stats[g, :, 128:256] = 1.0 / total

    def stats_copy(j):
        return block_copy(stats, g, (g + j) % N_GRP, st_send_sem, st_recv_sem, j)

    def start_stats(j, carry):
        stats_copy(j).start()
        return carry

    lax.fori_loop(1, N_GRP, start_stats, 0)

    def block_weights(block):
        return items_all[block, PER_ITEM:PAD_ITEM, 0:B_DEV].astype(jnp.float32)[1:2]

    group_sum = jnp.zeros((1, 1), jnp.float32)
    for b in range(N_GRP):
        group_sum = group_sum + jnp.sum(block_weights(b), axis=1, keepdims=True)
    ids1 = jnp.where(iota((16, 128), 1) == 2 * N_Y, group_sum, ids1)
    for k in range(N_Z):
        ids1_send[k] = ids1[k : k + 1]
    ids1_recv[z] = ids1_send[z]


    pl.semaphore_wait(z_sems.at[2], 2)
    pl.semaphore_wait(y_sems.at[1], 2)

    def ids1_copy(j):
        zt = (z + j) % N_Z
        return pltpu.make_async_remote_copy(
            src_ref=ids1_send.at[zt],
            dst_ref=ids1_recv.at[z],
            send_sem=i1_send_sem,
            recv_sem=i1_recv_sem,
            device_id={"dp": zt * N_Y + y},
            device_id_type=MESH,
        )

    def start_ids1(j, carry):
        ids1_copy(j).start()
        return carry

    lax.fori_loop(1, N_Z, start_ids1, 0)

    block_cross(behind_g)
    block_cross(ahead_g)
    block_cross(far_g)
    for other in (x, behind_x, ahead_x, far_x):
        block = 2 * other + 1 - c
        arrived(q_all, block, q_sems)
        block_cross(block)

    def wait_stats(j, carry):
        block_copy(stats, (g + j) % N_GRP, sib, st_send_sem, st_recv_sem, 0).wait_recv()
        return carry

    lax.fori_loop(1, N_GRP, wait_stats, 0)

    pos_sub, pos_lane = iota((PER_ITEM, B_DEV), 0), iota((PER_ITEM, B_DEV), 1)
    for b in range(N_GRP):
        share = jnp.exp(cross[b] - stats[b, :, 0:128]) * stats[b, :, 128:256]
        share = share - jnp.where(pos_sub + b * PER_ITEM == pos_lane + g * PER_ITEM, 1.0, 0.0)
        grads[:, b * B_DEV : (b + 1) * B_DEV] = (block_weights(b) * share).astype(jnp.bfloat16)
    item_grad = jnp.dot(
        grads[...], q_all[...].reshape(N_GRP * B_DEV, D), preferred_element_type=jnp.float32
    ).astype(jnp.bfloat16)
    placed = jnp.dot(slots[...], item_grad, preferred_element_type=jnp.float32)
    send1[...] = placed.astype(jnp.bfloat16).reshape(N_Z, 2 * N_Y, D)

    def rows1_copy(j):
        zt = (z + j) % N_Z
        return pltpu.make_async_remote_copy(
            src_ref=send1.at[zt],
            dst_ref=recv1.at[z],
            send_sem=r1_send_sem,
            recv_sem=r1_recv_sem,
            device_id={"dp": zt * N_Y + y},
            device_id_type=MESH,
        )

    def start_rows1(j, carry):
        rows1_copy(j).start()
        return carry

    lax.fori_loop(1, N_Z, start_rows1, 0)
    recv1[z] = send1[z]

    inverse = 1.0 / total
    for b in range(N_GRP):
        share = logits[b] * inverse
        share = share - jnp.where(pos_sub + b * PER_ITEM == pos_lane + g * PER_ITEM, 1.0, 0.0)
        probs[b, 0:PER_ITEM, :] = (weights * share).astype(jnp.bfloat16)
        probs[b, PER_ITEM:PAD_ITEM, :] = jnp.zeros((PAD_ITEM - PER_ITEM, B_DEV), jnp.bfloat16)
    query_grad = tn_dot(
        probs[...].reshape(N_GRP * PAD_ITEM, B_DEV), items_all[...].reshape(N_GRP * PAD_ITEM, D)
    )

    pltpu.make_async_copy(ids1_recv.at[pl.ds(0, N_Z - 1)], ids1_recv.at[pl.ds(0, N_Z - 1)], i1_recv_sem).wait()
    ids1_flat[...] = jnp.zeros((16, 128), jnp.float32)
    for k in range(N_Z):
        ids1_flat[k : k + 1, :] = ids1_recv[k]
    got1 = ids1_flat[...]
    y_sub, l_lane = iota((N_Y, 128), 0), iota((N_Y, 128), 1)
    z_sub, s_lane = iota((16, D), 0), iota((16, D), 1)
    ids2 = jnp.zeros((N_Y, D), jnp.float32)
    for k in range(2):
        pick = jnp.where(l_lane == 2 * y_sub + k, 1.0, 0.0)
        spread = jnp.where(s_lane == y * 32 + 2 * z_sub + k, 1.0, 0.0)
        picked = nt_dot(pick, got1, HIGHEST)
        ids2 = ids2 + jnp.dot(picked, spread, precision=HIGHEST, preferred_element_type=jnp.float32)
    summed = jnp.sum(got1, axis=0, keepdims=True)
    w_z = jnp.sum(jnp.where(iota((1, 128), 1) == 2 * N_Y, summed, 0.0), axis=1, keepdims=True)
    ids2 = jnp.where(iota((N_Y, D), 1) == y * 32 + 24, w_z, ids2)
    for k in range(N_Y):
        ids2_send[k] = ids2[k : k + 1]
    ids2_recv[y] = ids2_send[y]

    def ids2_copy(j):
        yt = (y + j) % N_Y
        return pltpu.make_async_remote_copy(
            src_ref=ids2_send.at[yt],
            dst_ref=ids2_recv.at[y],
            send_sem=i2_send_sem,
            recv_sem=i2_recv_sem,
            device_id={"dp": z * N_Y + yt},
            device_id_type=MESH,
        )

    def start_ids2(j, carry):
        ids2_copy(j).start()
        return carry

    lax.fori_loop(1, N_Y, start_ids2, 0)

    pltpu.make_async_copy(recv1.at[pl.ds(0, N_Z - 1)], recv1.at[pl.ds(0, N_Z - 1)], r1_recv_sem).wait()
    turned = jnp.dot(perm[...], recv1[...].reshape(2 * N_Z * N_Y, D), preferred_element_type=jnp.float32)
    send2[...] = turned.astype(jnp.bfloat16).reshape(N_Y, 32, D)

    def rows2_copy(j):
        yt = (y + j) % N_Y
        return pltpu.make_async_remote_copy(
            src_ref=send2.at[yt],
            dst_ref=recv2.at[y],
            send_sem=r2_send_sem,
            recv_sem=r2_recv_sem,
            device_id={"dp": z * N_Y + yt},
            device_id_type=MESH,
        )

    def start_rows2(j, carry):
        rows2_copy(j).start()
        return carry

    lax.fori_loop(1, N_Y, start_rows2, 0)
    recv2[y] = send2[y]

    pltpu.make_async_copy(ids2_recv.at[pl.ds(0, N_Y - 1)], ids2_recv.at[pl.ds(0, N_Y - 1)], i2_recv_sem).wait()
    got2 = ids2_recv[0]
    for k in range(1, N_Y):
        got2 = got2 + ids2_recv[k]
    in_block = iota((1, D), 1) % 32
    norm = BATCH / jnp.sum(jnp.where(in_block == 24, got2, 0.0), axis=1, keepdims=True)
    row_ids = jnp.where(in_block < 2 * N_Z, got2, 0.0).astype(jnp.int32)

    member[...] = jnp.where(iota((ROWS_DEV, D), 0) + 1 == row_ids, 1.0, 0.0).astype(jnp.bfloat16)
    dq_ref[...] = (query_grad * norm).astype(jnp.bfloat16)


    for copy in sent:
        copy.wait_send()
    def wait_stats_sent(j, carry):
        stats_copy(j).wait_send()
        return carry

    lax.fori_loop(1, N_GRP, wait_stats_sent, 0)
    pltpu.make_async_copy(ids1_send.at[pl.ds(0, N_Z - 1)], ids1_send.at[pl.ds(0, N_Z - 1)], i1_send_sem).wait()
    pltpu.make_async_copy(ids2_send.at[pl.ds(0, N_Y - 1)], ids2_send.at[pl.ds(0, N_Y - 1)], i2_send_sem).wait()
    pltpu.make_async_copy(send1.at[pl.ds(0, N_Z - 1)], send1.at[pl.ds(0, N_Z - 1)], r1_send_sem).wait()
    pltpu.make_async_copy(recv2.at[pl.ds(0, N_Y - 1)], recv2.at[pl.ds(0, N_Y - 1)], r2_recv_sem).wait()
    tab_ref[...] = norm * jnp.dot(
        member[...], recv2[...].reshape(N_Y * 32, D), preferred_element_type=jnp.float32
    )
    pltpu.make_async_copy(send2.at[pl.ds(0, N_Y - 1)], send2.at[pl.ds(0, N_Y - 1)], r2_send_sem).wait()


def shards(queries, item_vecs, log_q, weights, item_owner, item_row):
    vmem = pl.BlockSpec(memory_space=pltpu.VMEM)
    bf16, f32 = jnp.bfloat16, jnp.float32
    dma = pltpu.SemaphoreType.DMA
    return pl.pallas_call(
        kernel,
        out_shape=(
            jax.ShapeDtypeStruct((B_DEV, D), bf16),
            jax.ShapeDtypeStruct((ROWS_DEV, D), f32),
        ),
        in_specs=[pl.BlockSpec(memory_space=pltpu.HBM)] * 6,
        out_specs=(vmem, vmem),
        scratch_shapes=[
            pltpu.VMEM((PER_ITEM,), bf16),
            pltpu.VMEM((B_DEV,), bf16),
            pltpu.VMEM((1, PER_ITEM), jnp.int32),
            pltpu.VMEM((1, PER_ITEM), jnp.int32),
            pltpu.VMEM((N_GRP, PAD_ITEM, D), bf16),
            pltpu.VMEM((N_GRP, B_DEV, D), bf16),
            pltpu.VMEM((N_GRP, PER_ITEM, B_DEV), f32),
            pltpu.VMEM((N_GRP, PAD_ITEM, B_DEV), bf16),
            pltpu.VMEM((N_GRP, PER_ITEM, B_DEV), f32),
            pltpu.VMEM((PER_ITEM, N_GRP * B_DEV), bf16),
            pltpu.VMEM((N_GRP, 1, 256), f32),
            pltpu.VMEM((N_Z, 1, 128), f32),
            pltpu.VMEM((N_Z, 1, 128), f32),
            pltpu.VMEM((16, 128), f32),
            pltpu.VMEM((N_Y, 1, D), f32),
            pltpu.VMEM((N_Y, 1, D), f32),
            pltpu.VMEM((2 * N_Z * N_Y, PER_ITEM), bf16),
            pltpu.VMEM((N_Y * 32, 2 * N_Z * N_Y), bf16),
            pltpu.VMEM((ROWS_DEV, D), bf16),
            pltpu.VMEM((N_Z, 2 * N_Y, D), bf16),
            pltpu.VMEM((N_Z, 2 * N_Y, D), bf16),
            pltpu.VMEM((N_Y, 32, D), bf16),
            pltpu.VMEM((N_Y, 32, D), bf16),
            dma((6,)), pltpu.SemaphoreType.REGULAR((3,)), pltpu.SemaphoreType.REGULAR((2,)),
            dma((7,)), dma((N_GRP,)),
            dma((7,)), dma((N_GRP,)),
            dma((N_GRP,)), dma((N_GRP,)),
            dma, dma, dma, dma, dma, dma, dma, dma,
        ],
        compiler_params=pltpu.CompilerParams(
            collective_id=0, has_side_effects=True, vmem_limit_bytes=32 * 1024 * 1024
        ),
    )(*(
        pltpu.with_memory_space_constraint(operand, pltpu.HBM)
        for operand in (
            queries,
            item_vecs,
            log_q,
            weights,
            item_owner.reshape(1, PER_ITEM),
            item_row.reshape(1, PER_ITEM),
        )
    ))


def solution(mesh):
    in_specs = (
        P(("grp", "dp"), None),
        P(("grp", "dp"), None),
        P(("grp", "dp")),
        P(("grp", "dp")),
        P(("grp", "dp"), None),
        P(("grp", "dp")),
    )
    out_specs = (P(("grp", "dp"), None), P(("grp", "dp"), None))
    return jax.shard_map(shards, mesh=mesh, in_specs=in_specs, out_specs=out_specs, check_vma=False)
```

```python
import functools

import jax
import jax.numpy as jnp
from jax import lax
from jax.experimental import pallas as pl
from jax.experimental.pallas import tpu as pltpu
from jax.sharding import PartitionSpec as P

N_X = 4
N_GRP = 8
N_Z = 12
N_Y = 8
B_DEV = 128
PER_ITEM = 160
ROWS_DEV = 1024
D = 256
BATCH = 98304
MESH = pl.DeviceIdType.MESH
HIGHEST = lax.Precision.HIGHEST


def nt_dot(left, right, precision=None):
    return lax.dot_general(
        left, right, (((1,), (1,)), ((), ())), precision=precision, preferred_element_type=jnp.float32
    )


def tn_dot(left, right):
    return lax.dot_general(left, right, (((0,), (0,)), ((), ())), preferred_element_type=jnp.float32)


def iota(shape, dim):
    return lax.broadcasted_iota(jnp.int32, shape, dim)


def kernel(
    q_hbm, it_hbm, lq_hbm, w_hbm, own_hbm, row_hbm,
    dq_ref, tab_ref,
    lq_ref, w_ref, own_ref, row_ref,
    items, q_all, w_all, cross, grads, own_stats, stats, dq_keep, dq_send, dq_got, dq_terms, dq_in,
    ids1_send, ids1_recv, ids1_flat, ids2_send, ids2_recv,
    slots, perm, member, send1, recv1, send2, recv2,
    in_sem, z_sems, y_sems,
    q_send_sem, q_recv_sem, w_send_sem, w_recv_sem, st_send_sem, st_recv_sem,
    dp_send_sem, dp_recv_sem, dx_send_sem, dx_recv_sem,
    i1_send_sem, i1_recv_sem, i2_send_sem, i2_recv_sem,
    r1_send_sem, r1_recv_sem, r2_send_sem, r2_recv_sem,
):
    g = lax.axis_index("grp")
    d = lax.axis_index("dp")
    z, y = d // N_Y, d % N_Y
    x, c = g // 2, g % 2
    sib = 2 * x + 1 - c
    ahead = 1 - 2 * c

    loads = [
        pltpu.make_async_copy(src, dst, in_sem.at[i])
        for i, (src, dst) in enumerate((
            (it_hbm, items),
            (q_hbm, q_all.at[g]),
            (lq_hbm, lq_ref),
            (w_hbm, w_ref),
            (own_hbm, own_ref),
            (row_hbm, row_ref),
        ))
    ]
    for load in loads:
        load.start()

    barrier = pltpu.get_barrier_semaphore()

    def greet_grp(j, carry):
        pl.semaphore_signal(barrier, inc=1, device_id={"grp": (g + j) % N_GRP}, device_id_type=MESH)
        return carry

    lax.fori_loop(1, N_GRP, greet_grp, 0)

    def z_peer(step):
        return {"dp": ((z + step + N_Z) % N_Z) * N_Y + y}

    def y_peer(step):
        return {"dp": z * N_Y + (y + step + N_Y) % N_Y}

    def signal_pair(sem, peer, step):
        pl.semaphore_signal(sem, inc=1, device_id=peer(step), device_id_type=MESH)
        pl.semaphore_signal(sem, inc=1, device_id=peer(-step), device_id_type=MESH)

    signal_pair(barrier, z_peer, 1)
    signal_pair(barrier, y_peer, 1)

    for load in loads:
        load.wait()
    log_q = lq_ref[...].astype(jnp.float32).reshape(1, PER_ITEM)
    weights = w_ref[...].astype(jnp.float32).reshape(1, B_DEV)
    w_all[g] = weights

    pl.semaphore_wait(barrier, (N_GRP - 1) + 2 + 2)

    def block_copy(buf, block, target, send_sem, recv_sem, index):
        return pltpu.make_async_remote_copy(
            src_ref=buf.at[block],
            dst_ref=buf.at[block],
            send_sem=send_sem.at[index],
            recv_sem=recv_sem.at[block],
            device_id={"grp": target},
            device_id_type=MESH,
        )

    def chip(dx):
        return (x + dx + N_X) % N_X

    behind_x, ahead_x, far_x = chip(-ahead), chip(ahead), chip(2)
    behind_g, ahead_g, far_g = 2 * behind_x + c, 2 * ahead_x + c, 2 * far_x + c
    sent = []

    def send(buf, block, target, sems, index):
        copy = block_copy(buf, block, target, sems[0], sems[1], index)
        copy.start()
        sent.append(copy)

    def arrived(buf, block, sems):
        block_copy(buf, block, sib, sems[0], sems[1], 0).wait_recv()

    q_sems = (q_send_sem, q_recv_sem)

    def first_sends(buf, sems):
        send(buf, g, ahead_g, sems, 0)
        send(buf, g, behind_g, sems, 1)
        send(buf, g, sib, sems, 2)

    first_sends(q_all, q_sems)

    def weights_copy(j):
        return block_copy(w_all, g, (g + j) % N_GRP, w_send_sem, w_recv_sem, j)

    def start_weights(j, carry):
        weights_copy(j).start()
        return carry

    lax.fori_loop(1, N_GRP, start_weights, 0)
    signal_pair(z_sems.at[0], z_peer, 1)
    signal_pair(y_sems.at[0], y_peer, 1)

    owner_i = own_ref[...]
    row_i = row_ref[...]

    owner = owner_i.astype(jnp.float32)
    sub, lane = iota((PER_ITEM, PER_ITEM), 0), iota((PER_ITEM, PER_ITEM), 1)
    eye = sub == lane
    owner_col = jnp.sum(jnp.where(eye, owner, 0.0), axis=1, keepdims=True)
    lq_col = jnp.sum(jnp.where(eye, log_q, 0.0), axis=1, keepdims=True)
    same = jnp.where((owner_col == owner) & (sub < lane), 1.0, 0.0)
    place = jnp.sum(same, axis=0, keepdims=True).astype(jnp.int32)
    dest_z = owner_i // N_Y
    slot = owner_i * 2 + place
    slot_z = slot - dest_z * (2 * N_Y)

    kind = iota((48, PER_ITEM), 0) // 16
    sub48 = iota((48, PER_ITEM), 0) % 16
    part = jnp.where(kind == 0, row_i // 32, jnp.where(kind == 1, row_i % 32, 1)).astype(jnp.float32)
    left = jnp.where(sub48 == dest_z, part, 0.0).astype(jnp.bfloat16)
    right = jnp.where(iota((128, PER_ITEM), 0) == slot_z, 1.0, 0.0).astype(jnp.bfloat16)
    found = nt_dot(left, right)
    ids1 = found[0:16] * 32.0 + found[16:32] + found[32:48]

    slots[...] = jnp.where(iota((2 * N_Z * N_Y, PER_ITEM), 0) == slot, 1.0, 0.0).astype(jnp.bfloat16)
    pr, pc = iota((N_Y * 32, 2 * N_Z * N_Y), 0), iota((N_Y * 32, 2 * N_Z * N_Y), 1)
    in_y = pr % 32
    perm[...] = jnp.where(
        (in_y < 2 * N_Z) & (pc == (in_y // 2) * (2 * N_Y) + (pr // 32) * 2 + in_y % 2), 1.0, 0.0
    ).astype(jnp.bfloat16)

    def block_logits(block):
        value = nt_dot(items[...], q_all[block]) - lq_col
        top = jnp.max(value, axis=0, keepdims=True)
        shifted = jnp.exp(value - top)
        cross[block] = shifted
        own_stats[block, :, 0:128] = top
        own_stats[block, :, 128:256] = jnp.sum(shifted, axis=0, keepdims=True)

    def other_core(chip_x):
        return 2 * chip_x + 1 - c

    block_logits(g)
    arrived(q_all, sib, q_sems)
    block_logits(sib)
    arrived(q_all, behind_g, q_sems)
    send(q_all, behind_g, ahead_g, q_sems, 3)
    send(q_all, behind_g, sib, q_sems, 4)
    arrived(q_all, ahead_g, q_sems)
    send(q_all, ahead_g, sib, q_sems, 5)
    pl.semaphore_wait(z_sems.at[0], 2)
    signal_pair(z_sems.at[1], z_peer, 2)
    pl.semaphore_wait(y_sems.at[0], 2)
    signal_pair(y_sems.at[1], y_peer, 2)
    block_logits(behind_g)
    block_logits(ahead_g)
    arrived(q_all, far_g, q_sems)
    send(q_all, far_g, sib, q_sems, 6)
    arrived(q_all, other_core(behind_x), q_sems)
    block_logits(other_core(behind_x))
    arrived(q_all, other_core(ahead_x), q_sems)
    block_logits(other_core(ahead_x))
    block_logits(far_g)
    pl.semaphore_wait(z_sems.at[1], 2)
    signal_pair(z_sems.at[2], z_peer, 2)
    arrived(q_all, other_core(far_x), q_sems)
    block_logits(other_core(far_x))

    for b in range(N_GRP):
        stats[g, b : b + 1, :] = own_stats[b]

    def stats_copy(j):
        return block_copy(stats, g, (g + j) % N_GRP, st_send_sem, st_recv_sem, j)

    def start_stats(j, carry):
        stats_copy(j).start()
        return carry

    lax.fori_loop(1, N_GRP, start_stats, 0)

    def wait_weights(j, carry):
        block_copy(w_all, (g + j) % N_GRP, sib, w_send_sem, w_recv_sem, 0).wait_recv()
        return carry

    lax.fori_loop(1, N_GRP, wait_weights, 0)
    all_weights = w_all[0]
    for b in range(1, N_GRP):
        all_weights = all_weights + w_all[b]
    group_sum = jnp.sum(all_weights, axis=1, keepdims=True)
    ids1 = jnp.where(iota((16, 128), 1) == 2 * N_Y, group_sum, ids1)
    for k in range(N_Z):
        ids1_send[k] = ids1[k : k + 1]
    ids1_recv[z] = ids1_send[z]

    pl.semaphore_wait(y_sems.at[1], 2)
    pl.semaphore_wait(z_sems.at[2], 2)

    def ids1_copy(j):
        zt = (z + j) % N_Z
        return pltpu.make_async_remote_copy(
            src_ref=ids1_send.at[zt],
            dst_ref=ids1_recv.at[z],
            send_sem=i1_send_sem,
            recv_sem=i1_recv_sem,
            device_id={"dp": zt * N_Y + y},
            device_id_type=MESH,
        )

    def start_ids1(j, carry):
        ids1_copy(j).start()
        return carry

    lax.fori_loop(1, N_Z, start_ids1, 0)

    def wait_stats(j, carry):
        block_copy(stats, (g + j) % N_GRP, sib, st_send_sem, st_recv_sem, 0).wait_recv()
        return carry

    lax.fori_loop(1, N_GRP, wait_stats, 0)

    tops = [stats[b, :, 0:128] for b in range(N_GRP)]
    top = functools.reduce(jnp.maximum, tops)
    total = jnp.zeros((N_GRP, B_DEV), jnp.float32)
    for b in range(N_GRP):
        total = total + jnp.exp(tops[b] - top) * stats[b, :, 128:256]
    scale = jnp.exp(stats[g, :, 0:128] - top) / total
    pos_sub, pos_lane = iota((PER_ITEM, B_DEV), 0), iota((PER_ITEM, B_DEV), 1)
    for b in range(N_GRP):
        share = cross[b] * scale[b : b + 1]
        share = share - jnp.where(pos_sub + b * PER_ITEM == pos_lane + g * PER_ITEM, 1.0, 0.0)
        grads[:, b * B_DEV : (b + 1) * B_DEV] = (w_all[b] * share).astype(jnp.bfloat16)
    item_grad = jnp.dot(
        grads[...], q_all[...].reshape(N_GRP * B_DEV, D), preferred_element_type=jnp.float32
    ).astype(jnp.bfloat16)
    placed = jnp.dot(slots[...], item_grad, preferred_element_type=jnp.float32)
    send1[...] = placed.astype(jnp.bfloat16).reshape(N_Z, 2 * N_Y, D)

    def rows1_copy(j):
        zt = (z + j) % N_Z
        return pltpu.make_async_remote_copy(
            src_ref=send1.at[zt],
            dst_ref=recv1.at[z],
            send_sem=r1_send_sem,
            recv_sem=r1_recv_sem,
            device_id={"dp": zt * N_Y + y},
            device_id_type=MESH,
        )

    def start_rows1(j, carry):
        rows1_copy(j).start()
        return carry

    lax.fori_loop(1, N_Z, start_rows1, 0)
    recv1[z] = send1[z]

    def query_term(block):
        columns = pl.ds(pl.multiple_of(block * B_DEV, B_DEV), B_DEV)
        return tn_dot(grads[:, columns], items[...])

    def pair_copy(k):
        return pltpu.make_async_remote_copy(
            src_ref=dq_send.at[k],
            dst_ref=dq_got.at[k],
            send_sem=dp_send_sem.at[k],
            recv_sem=dp_recv_sem.at[k],
            device_id={"grp": sib},
            device_id_type=MESH,
        )

    for k in range(N_X):
        dq_send[k] = query_term(2 * chip(k) + 1 - c)
        pair_copy(k).start()
    for k in range(N_X):
        dq_keep[k] = query_term(2 * chip(k) + c)

    pltpu.make_async_copy(ids1_recv.at[pl.ds(0, N_Z - 1)], ids1_recv.at[pl.ds(0, N_Z - 1)], i1_recv_sem).wait()
    ids1_flat[...] = jnp.zeros((16, 128), jnp.float32)
    for k in range(N_Z):
        ids1_flat[k : k + 1, :] = ids1_recv[k]
    got1 = ids1_flat[...]
    y_sub, l_lane = iota((N_Y, 128), 0), iota((N_Y, 128), 1)
    z_sub, s_lane = iota((16, D), 0), iota((16, D), 1)
    ids2 = jnp.zeros((N_Y, D), jnp.float32)
    for k in range(2):
        pick = jnp.where(l_lane == 2 * y_sub + k, 1.0, 0.0)
        spread = jnp.where(s_lane == y * 32 + 2 * z_sub + k, 1.0, 0.0)
        picked = nt_dot(pick, got1, HIGHEST)
        ids2 = ids2 + jnp.dot(picked, spread, precision=HIGHEST, preferred_element_type=jnp.float32)
    summed = jnp.sum(got1, axis=0, keepdims=True)
    w_z = jnp.sum(jnp.where(iota((1, 128), 1) == 2 * N_Y, summed, 0.0), axis=1, keepdims=True)
    ids2 = jnp.where(iota((N_Y, D), 1) == y * 32 + 24, w_z, ids2)
    for k in range(N_Y):
        ids2_send[k] = ids2[k : k + 1]
    ids2_recv[y] = ids2_send[y]

    def ids2_copy(j):
        yt = (y + j) % N_Y
        return pltpu.make_async_remote_copy(
            src_ref=ids2_send.at[yt],
            dst_ref=ids2_recv.at[y],
            send_sem=i2_send_sem,
            recv_sem=i2_recv_sem,
            device_id={"dp": z * N_Y + yt},
            device_id_type=MESH,
        )

    def start_ids2(j, carry):
        ids2_copy(j).start()
        return carry

    lax.fori_loop(1, N_Y, start_ids2, 0)

    def chip_copy(k):
        return pltpu.make_async_remote_copy(
            src_ref=dq_terms.at[k],
            dst_ref=dq_in.at[k],
            send_sem=dx_send_sem.at[k],
            recv_sem=dx_recv_sem.at[k],
            device_id={"grp": 2 * chip(k) + c},
            device_id_type=MESH,
        )

    for k in (2, 1, 3):
        pair_copy(k).wait_recv()
        dq_terms[k] = (dq_keep[k] + dq_got[k]).astype(jnp.bfloat16)
        chip_copy(k).start()
    pair_copy(0).wait_recv()

    pltpu.make_async_copy(recv1.at[pl.ds(0, N_Z - 1)], recv1.at[pl.ds(0, N_Z - 1)], r1_recv_sem).wait()
    turned = jnp.dot(perm[...], recv1[...].reshape(2 * N_Z * N_Y, D), preferred_element_type=jnp.float32)
    send2[...] = turned.astype(jnp.bfloat16).reshape(N_Y, 32, D)

    def rows2_copy(j):
        yt = (y + j) % N_Y
        return pltpu.make_async_remote_copy(
            src_ref=send2.at[yt],
            dst_ref=recv2.at[y],
            send_sem=r2_send_sem,
            recv_sem=r2_recv_sem,
            device_id={"dp": z * N_Y + yt},
            device_id_type=MESH,
        )

    def start_rows2(j, carry):
        rows2_copy(j).start()
        return carry

    lax.fori_loop(1, N_Y, start_rows2, 0)
    recv2[y] = send2[y]

    pltpu.make_async_copy(ids2_recv.at[pl.ds(0, N_Y - 1)], ids2_recv.at[pl.ds(0, N_Y - 1)], i2_recv_sem).wait()
    got2 = ids2_recv[0]
    for k in range(1, N_Y):
        got2 = got2 + ids2_recv[k]
    in_block = iota((1, D), 1) % 32
    norm = BATCH / jnp.sum(jnp.where(in_block == 24, got2, 0.0), axis=1, keepdims=True)
    row_ids = jnp.where(in_block < 2 * N_Z, got2, 0.0).astype(jnp.int32)

    member[...] = jnp.where(iota((ROWS_DEV, D), 0) + 1 == row_ids, 1.0, 0.0).astype(jnp.bfloat16)
    query_grad = dq_keep[0] + dq_got[0]
    for k in (1, 3, 2):
        chip_copy(k).wait_recv()
        query_grad = query_grad + dq_in[k].astype(jnp.float32)
    dq_ref[...] = (query_grad * norm).astype(jnp.bfloat16)


    for copy in sent:
        copy.wait_send()
    for k in range(N_X):
        pair_copy(k).wait_send()
    for k in range(1, N_X):
        chip_copy(k).wait_send()
    def wait_stats_sent(j, carry):
        stats_copy(j).wait_send()
        weights_copy(j).wait_send()
        return carry

    lax.fori_loop(1, N_GRP, wait_stats_sent, 0)
    pltpu.make_async_copy(ids1_send.at[pl.ds(0, N_Z - 1)], ids1_send.at[pl.ds(0, N_Z - 1)], i1_send_sem).wait()
    pltpu.make_async_copy(ids2_send.at[pl.ds(0, N_Y - 1)], ids2_send.at[pl.ds(0, N_Y - 1)], i2_send_sem).wait()
    pltpu.make_async_copy(send1.at[pl.ds(0, N_Z - 1)], send1.at[pl.ds(0, N_Z - 1)], r1_send_sem).wait()
    pltpu.make_async_copy(recv2.at[pl.ds(0, N_Y - 1)], recv2.at[pl.ds(0, N_Y - 1)], r2_recv_sem).wait()
    tab_ref[...] = norm * jnp.dot(
        member[...], recv2[...].reshape(N_Y * 32, D), preferred_element_type=jnp.float32
    )
    pltpu.make_async_copy(send2.at[pl.ds(0, N_Y - 1)], send2.at[pl.ds(0, N_Y - 1)], r2_send_sem).wait()


def shards(queries, item_vecs, log_q, weights, item_owner, item_row):
    vmem = pl.BlockSpec(memory_space=pltpu.VMEM)
    bf16, f32 = jnp.bfloat16, jnp.float32
    dma = pltpu.SemaphoreType.DMA
    return pl.pallas_call(
        kernel,
        out_shape=(
            jax.ShapeDtypeStruct((B_DEV, D), bf16),
            jax.ShapeDtypeStruct((ROWS_DEV, D), f32),
        ),
        in_specs=[pl.BlockSpec(memory_space=pltpu.HBM)] * 6,
        out_specs=(vmem, vmem),
        scratch_shapes=[
            pltpu.VMEM((PER_ITEM,), bf16),
            pltpu.VMEM((B_DEV,), bf16),
            pltpu.VMEM((1, PER_ITEM), jnp.int32),
            pltpu.VMEM((1, PER_ITEM), jnp.int32),
            pltpu.VMEM((PER_ITEM, D), bf16),
            pltpu.VMEM((N_GRP, B_DEV, D), bf16),
            pltpu.VMEM((N_GRP, 1, B_DEV), f32),
            pltpu.VMEM((N_GRP, PER_ITEM, B_DEV), f32),
            pltpu.VMEM((PER_ITEM, N_GRP * B_DEV), bf16),
            pltpu.VMEM((N_GRP, 1, 256), f32),
            pltpu.VMEM((N_GRP, N_GRP, 256), f32),
            pltpu.VMEM((N_X, B_DEV, D), f32),
            pltpu.VMEM((N_X, B_DEV, D), f32),
            pltpu.VMEM((N_X, B_DEV, D), f32),
            pltpu.VMEM((N_X, B_DEV, D), bf16),
            pltpu.VMEM((N_X, B_DEV, D), bf16),
            pltpu.VMEM((N_Z, 1, 128), f32),
            pltpu.VMEM((N_Z, 1, 128), f32),
            pltpu.VMEM((16, 128), f32),
            pltpu.VMEM((N_Y, 1, D), f32),
            pltpu.VMEM((N_Y, 1, D), f32),
            pltpu.VMEM((2 * N_Z * N_Y, PER_ITEM), bf16),
            pltpu.VMEM((N_Y * 32, 2 * N_Z * N_Y), bf16),
            pltpu.VMEM((ROWS_DEV, D), bf16),
            pltpu.VMEM((N_Z, 2 * N_Y, D), bf16),
            pltpu.VMEM((N_Z, 2 * N_Y, D), bf16),
            pltpu.VMEM((N_Y, 32, D), bf16),
            pltpu.VMEM((N_Y, 32, D), bf16),
            dma((6,)), pltpu.SemaphoreType.REGULAR((3,)), pltpu.SemaphoreType.REGULAR((2,)),
            dma((7,)), dma((N_GRP,)),
            dma((N_GRP,)), dma((N_GRP,)),
            dma((N_GRP,)), dma((N_GRP,)),
            dma((N_X,)), dma((N_X,)), dma((N_X,)), dma((N_X,)),
            dma, dma, dma, dma, dma, dma, dma, dma,
        ],
        compiler_params=pltpu.CompilerParams(
            collective_id=0, has_side_effects=True, vmem_limit_bytes=32 * 1024 * 1024
        ),
    )(*(
        pltpu.with_memory_space_constraint(operand, pltpu.HBM)
        for operand in (
            queries,
            item_vecs,
            log_q,
            weights,
            item_owner.reshape(1, PER_ITEM),
            item_row.reshape(1, PER_ITEM),
        )
    ))


def solution(mesh):
    in_specs = (
        P(("grp", "dp"), None),
        P(("grp", "dp"), None),
        P(("grp", "dp")),
        P(("grp", "dp")),
        P(("grp", "dp"), None),
        P(("grp", "dp")),
    )
    out_specs = (P(("grp", "dp"), None), P(("grp", "dp"), None))
    return jax.shard_map(shards, mesh=mesh, in_specs=in_specs, out_specs=out_specs, check_vma=False)
```

```python
import functools

import jax
import jax.numpy as jnp
from jax import lax
from jax.experimental import pallas as pl
from jax.experimental.pallas import tpu as pltpu
from jax.sharding import PartitionSpec as P

N_X = 4
N_GRP = 8
N_Z = 12
N_Y = 8
B_DEV = 128
Q_ROWS = 144
PER_ITEM = 160
ROWS_DEV = 1024
D = 256
BATCH = 98304
Z_ORDER = (6, 5, 7, 4, 8, 3, 9, 2, 10, 1, 11)
Y_ORDER = (4, 3, 5, 2, 6, 1, 7)
MESH = pl.DeviceIdType.MESH
HIGHEST = lax.Precision.HIGHEST


def nt_dot(left, right, precision=None):
    return lax.dot_general(
        left, right, (((1,), (1,)), ((), ())), precision=precision, preferred_element_type=jnp.float32
    )


def tn_dot(left, right):
    return lax.dot_general(left, right, (((0,), (0,)), ((), ())), preferred_element_type=jnp.float32)


def iota(shape, dim):
    return lax.broadcasted_iota(jnp.int32, shape, dim)


def kernel(
    q_hbm, it_hbm, lq_hbm, w_hbm, own_hbm, row_hbm,
    dq_ref, tab_ref,
    lq_ref, w_ref, own_ref, row_ref,
    items, q_all, cross, grads, own_stats, stats, dq_keep, dq_send, dq_got, dq_terms, dq_in,
    ids1_send, ids1_recv, ids1_flat, ids2_send, ids2_recv,
    slots, perm, member, send1, recv1, send2, recv2,
    in_sem, z_sems, y_sems,
    q_send_sem, q_recv_sem, st_send_sem, st_recv_sem,
    dp_send_sem, dp_recv_sem, dx_send_sem, dx_recv_sem,
    i1_send_sem, i1_recv_sem, i2_send_sem, i2_recv_sem,
    r1_send_sem, r1_recv_sem, r2_send_sem, r2_recv_sem,
):
    g = lax.axis_index("grp")
    d = lax.axis_index("dp")
    z, y = d // N_Y, d % N_Y
    x, c = g // 2, g % 2
    sib = 2 * x + 1 - c
    ahead = 1 - 2 * c

    loads = [
        pltpu.make_async_copy(src, dst, in_sem.at[i])
        for i, (src, dst) in enumerate((
            (it_hbm, items),
            (q_hbm, q_all.at[g, pl.ds(0, B_DEV)]),
            (lq_hbm, lq_ref),
            (w_hbm, w_ref),
            (own_hbm, own_ref),
            (row_hbm, row_ref),
        ))
    ]
    for load in loads:
        load.start()

    barrier = pltpu.get_barrier_semaphore()

    def chip(dx):
        return (x + dx + N_X) % N_X

    behind_x, ahead_x, far_x = chip(-ahead), chip(ahead), chip(2)
    behind_g, ahead_g, far_g = 2 * behind_x + c, 2 * ahead_x + c, 2 * far_x + c
    for peer in (ahead_g, behind_g, sib, far_g):
        pl.semaphore_signal(barrier, inc=1, device_id={"grp": peer}, device_id_type=MESH)

    def z_peer(step):
        return {"dp": ((z + step + N_Z) % N_Z) * N_Y + y}

    def y_peer(step):
        return {"dp": z * N_Y + (y + step + N_Y) % N_Y}

    def signal_pair(sem, peer, step):
        pl.semaphore_signal(sem, inc=1, device_id=peer(step), device_id_type=MESH)
        pl.semaphore_signal(sem, inc=1, device_id=peer(-step), device_id_type=MESH)

    signal_pair(barrier, z_peer, 1)
    signal_pair(barrier, y_peer, 1)

    for load in loads:
        load.wait()
    log_q = lq_ref[...].astype(jnp.float32).reshape(1, PER_ITEM)
    weights = w_ref[...].astype(jnp.float32).reshape(1, B_DEV)
    padded_w = jnp.concatenate([weights, jnp.zeros((1, D - B_DEV), jnp.float32)], axis=1)
    q_all[g, B_DEV:Q_ROWS, :] = jnp.broadcast_to(padded_w, (Q_ROWS - B_DEV, D)).astype(jnp.bfloat16)

    pl.semaphore_wait(barrier, 4 + 2 + 2)

    def block_copy(buf, block, target, send_sem, recv_sem, index):
        return pltpu.make_async_remote_copy(
            src_ref=buf.at[block],
            dst_ref=buf.at[block],
            send_sem=send_sem.at[index],
            recv_sem=recv_sem.at[block],
            device_id={"grp": target},
            device_id_type=MESH,
        )

    sent = []

    def send(buf, block, target, sems, index):
        copy = block_copy(buf, block, target, sems[0], sems[1], index)
        copy.start()
        sent.append(copy)

    def arrived(buf, block, sems):
        block_copy(buf, block, sib, sems[0], sems[1], 0).wait_recv()

    q_sems = (q_send_sem, q_recv_sem)

    def first_sends(buf, sems):
        send(buf, g, far_g, sems, 3)
        send(buf, g, ahead_g, sems, 0)
        send(buf, g, behind_g, sems, 1)
        send(buf, g, sib, sems, 2)

    first_sends(q_all, q_sems)

    signal_pair(z_sems.at[0], z_peer, 1)
    signal_pair(y_sems.at[0], y_peer, 1)

    owner_i = own_ref[...]
    row_i = row_ref[...]

    owner = owner_i.astype(jnp.float32)
    sub, lane = iota((PER_ITEM, PER_ITEM), 0), iota((PER_ITEM, PER_ITEM), 1)
    eye = sub == lane
    owner_col = jnp.sum(jnp.where(eye, owner, 0.0), axis=1, keepdims=True)
    lq_col = jnp.sum(jnp.where(eye, log_q, 0.0), axis=1, keepdims=True)
    same = jnp.where((owner_col == owner) & (sub < lane), 1.0, 0.0)
    place = jnp.sum(same, axis=0, keepdims=True).astype(jnp.int32)
    dest_z = owner_i // N_Y
    slot = owner_i * 2 + place
    slot_z = slot - dest_z * (2 * N_Y)

    kind = iota((48, PER_ITEM), 0) // 16
    sub48 = iota((48, PER_ITEM), 0) % 16
    part = jnp.where(kind == 0, row_i // 32, jnp.where(kind == 1, row_i % 32, 1)).astype(jnp.float32)
    left = jnp.where(sub48 == dest_z, part, 0.0).astype(jnp.bfloat16)
    right = jnp.where(iota((128, PER_ITEM), 0) == slot_z, 1.0, 0.0).astype(jnp.bfloat16)
    found = nt_dot(left, right)
    ids1 = found[0:16] * 32.0 + found[16:32] + found[32:48]

    slots[...] = jnp.where(iota((2 * N_Z * N_Y, PER_ITEM), 0) == slot, 1.0, 0.0).astype(jnp.bfloat16)
    pr, pc = iota((N_Y * 32, 2 * N_Z * N_Y), 0), iota((N_Y * 32, 2 * N_Z * N_Y), 1)
    in_y = pr % 32
    perm[...] = jnp.where(
        (in_y < 2 * N_Z) & (pc == (in_y // 2) * (2 * N_Y) + (pr // 32) * 2 + in_y % 2), 1.0, 0.0
    ).astype(jnp.bfloat16)

    def block_logits(block):
        value = nt_dot(items[...], q_all[block, 0:B_DEV, :]) - lq_col
        top = jnp.max(value, axis=0, keepdims=True)
        shifted = jnp.exp(value - top)
        cross[block] = shifted
        own_stats[block, :, 0:128] = top
        own_stats[block, :, 128:256] = jnp.sum(shifted, axis=0, keepdims=True)

    def other_core(chip_x):
        return 2 * chip_x + 1 - c

    block_logits(g)
    arrived(q_all, sib, q_sems)
    block_logits(sib)
    arrived(q_all, behind_g, q_sems)
    send(q_all, behind_g, sib, q_sems, 4)
    arrived(q_all, ahead_g, q_sems)
    send(q_all, ahead_g, sib, q_sems, 5)
    pl.semaphore_wait(z_sems.at[0], 2)
    signal_pair(z_sems.at[1], z_peer, 2)
    pl.semaphore_wait(y_sems.at[0], 2)
    signal_pair(y_sems.at[1], y_peer, 2)
    block_logits(behind_g)
    block_logits(ahead_g)
    arrived(q_all, far_g, q_sems)
    send(q_all, far_g, sib, q_sems, 6)
    arrived(q_all, other_core(behind_x), q_sems)
    block_logits(other_core(behind_x))
    arrived(q_all, other_core(ahead_x), q_sems)
    block_logits(other_core(ahead_x))
    block_logits(far_g)
    pl.semaphore_wait(z_sems.at[1], 2)
    signal_pair(z_sems.at[2], z_peer, 2)
    arrived(q_all, other_core(far_x), q_sems)
    block_logits(other_core(far_x))

    for b in range(N_GRP):
        stats[g, b : b + 1, :] = own_stats[b]

    others = (
        far_g, other_core(far_x), ahead_g, behind_g, other_core(ahead_x), other_core(behind_x), sib
    )

    def stats_copy(j):
        return block_copy(stats, g, others[j], st_send_sem, st_recv_sem, j)

    for j in range(N_GRP - 1):
        stats_copy(j).start()

    block_weights = [q_all[b, B_DEV:Q_ROWS, 0:B_DEV].astype(jnp.float32)[0:1] for b in range(N_GRP)]
    all_weights = block_weights[0]
    for b in range(1, N_GRP):
        all_weights = all_weights + block_weights[b]
    group_sum = jnp.sum(all_weights, axis=1, keepdims=True)
    ids1 = jnp.where(iota((16, 128), 1) == 2 * N_Y, group_sum, ids1)
    for k in range(N_Z):
        ids1_send[k] = ids1[k : k + 1]
    ids1_recv[z] = ids1_send[z]

    pl.semaphore_wait(y_sems.at[1], 2)
    pl.semaphore_wait(z_sems.at[2], 2)

    def ids1_copy(j):
        zt = jnp.where(z + j >= N_Z, z + j - N_Z, z + j)
        return pltpu.make_async_remote_copy(
            src_ref=ids1_send.at[zt],
            dst_ref=ids1_recv.at[z],
            send_sem=i1_send_sem,
            recv_sem=i1_recv_sem,
            device_id={"dp": zt * N_Y + y},
            device_id_type=MESH,
        )

    for j in Z_ORDER:
        ids1_copy(j).start()

    for other in others:
        block_copy(stats, other, sib, st_send_sem, st_recv_sem, 0).wait_recv()

    tops = [stats[b, :, 0:128] for b in range(N_GRP)]
    top = functools.reduce(jnp.maximum, tops)
    total = jnp.zeros((N_GRP, B_DEV), jnp.float32)
    for b in range(N_GRP):
        total = total + jnp.exp(tops[b] - top) * stats[b, :, 128:256]
    scale = jnp.exp(stats[g, :, 0:128] - top) / total
    pos_sub, pos_lane = iota((PER_ITEM, B_DEV), 0), iota((PER_ITEM, B_DEV), 1)
    for b in range(N_GRP):
        share = cross[b] * scale[b : b + 1]
        share = share - jnp.where(pos_sub + b * PER_ITEM == pos_lane + g * PER_ITEM, 1.0, 0.0)
        grads[:, b * B_DEV : (b + 1) * B_DEV] = (block_weights[b] * share).astype(jnp.bfloat16)
    item_grad = jnp.dot(
        grads[...], q_all[:, 0:B_DEV, :].reshape(N_GRP * B_DEV, D), preferred_element_type=jnp.float32
    ).astype(jnp.bfloat16)
    placed = jnp.dot(slots[...], item_grad, preferred_element_type=jnp.float32)
    send1[...] = placed.astype(jnp.bfloat16).reshape(N_Z, 2 * N_Y, D)

    def rows1_copy(j):
        zt = jnp.where(z + j >= N_Z, z + j - N_Z, z + j)
        return pltpu.make_async_remote_copy(
            src_ref=send1.at[zt],
            dst_ref=recv1.at[z],
            send_sem=r1_send_sem,
            recv_sem=r1_recv_sem,
            device_id={"dp": zt * N_Y + y},
            device_id_type=MESH,
        )

    for j in Z_ORDER:
        rows1_copy(j).start()
    recv1[z] = send1[z]

    def query_term(block):
        columns = pl.ds(pl.multiple_of(block * B_DEV, B_DEV), B_DEV)
        return tn_dot(grads[:, columns], items[...])

    def pair_copy(k):
        return pltpu.make_async_remote_copy(
            src_ref=dq_send.at[k],
            dst_ref=dq_got.at[k],
            send_sem=dp_send_sem.at[k],
            recv_sem=dp_recv_sem.at[k],
            device_id={"grp": sib},
            device_id_type=MESH,
        )

    for k in range(N_X):
        dq_send[k] = query_term(2 * chip(k) + 1 - c)
        pair_copy(k).start()
    for k in range(N_X):
        dq_keep[k] = query_term(2 * chip(k) + c)

    pltpu.make_async_copy(ids1_recv.at[pl.ds(0, N_Z - 1)], ids1_recv.at[pl.ds(0, N_Z - 1)], i1_recv_sem).wait()
    ids1_flat[...] = jnp.zeros((16, 128), jnp.float32)
    for k in range(N_Z):
        ids1_flat[k : k + 1, :] = ids1_recv[k]
    got1 = ids1_flat[...]
    y_sub, l_lane = iota((N_Y, 128), 0), iota((N_Y, 128), 1)
    z_sub, s_lane = iota((16, D), 0), iota((16, D), 1)
    ids2 = jnp.zeros((N_Y, D), jnp.float32)
    for k in range(2):
        pick = jnp.where(l_lane == 2 * y_sub + k, 1.0, 0.0)
        spread = jnp.where(s_lane == y * 32 + 2 * z_sub + k, 1.0, 0.0)
        picked = nt_dot(pick, got1, HIGHEST)
        ids2 = ids2 + jnp.dot(picked, spread, precision=HIGHEST, preferred_element_type=jnp.float32)
    summed = jnp.sum(got1, axis=0, keepdims=True)
    w_z = jnp.sum(jnp.where(iota((1, 128), 1) == 2 * N_Y, summed, 0.0), axis=1, keepdims=True)
    ids2 = jnp.where(iota((N_Y, D), 1) == y * 32 + 24, w_z, ids2)
    for k in range(N_Y):
        ids2_send[k] = ids2[k : k + 1]
    ids2_recv[y] = ids2_send[y]

    def ids2_copy(j):
        yt = jnp.where(y + j >= N_Y, y + j - N_Y, y + j)
        return pltpu.make_async_remote_copy(
            src_ref=ids2_send.at[yt],
            dst_ref=ids2_recv.at[y],
            send_sem=i2_send_sem,
            recv_sem=i2_recv_sem,
            device_id={"dp": z * N_Y + yt},
            device_id_type=MESH,
        )

    for j in Y_ORDER:
        ids2_copy(j).start()

    def chip_copy(k):
        return pltpu.make_async_remote_copy(
            src_ref=dq_terms.at[k],
            dst_ref=dq_in.at[k],
            send_sem=dx_send_sem.at[k],
            recv_sem=dx_recv_sem.at[k],
            device_id={"grp": 2 * chip(k) + c},
            device_id_type=MESH,
        )

    for k in (2, 1, 3):
        pair_copy(k).wait_recv()
        dq_terms[k] = (dq_keep[k] + dq_got[k]).astype(jnp.bfloat16)
        chip_copy(k).start()
    pair_copy(0).wait_recv()

    pltpu.make_async_copy(recv1.at[pl.ds(0, N_Z - 1)], recv1.at[pl.ds(0, N_Z - 1)], r1_recv_sem).wait()
    turned = jnp.dot(perm[...], recv1[...].reshape(2 * N_Z * N_Y, D), preferred_element_type=jnp.float32)
    send2[...] = turned.astype(jnp.bfloat16).reshape(N_Y, 32, D)

    def rows2_copy(j):
        yt = jnp.where(y + j >= N_Y, y + j - N_Y, y + j)
        return pltpu.make_async_remote_copy(
            src_ref=send2.at[yt],
            dst_ref=recv2.at[y],
            send_sem=r2_send_sem,
            recv_sem=r2_recv_sem,
            device_id={"dp": z * N_Y + yt},
            device_id_type=MESH,
        )

    for j in Y_ORDER:
        rows2_copy(j).start()
    recv2[y] = send2[y]

    pltpu.make_async_copy(ids2_recv.at[pl.ds(0, N_Y - 1)], ids2_recv.at[pl.ds(0, N_Y - 1)], i2_recv_sem).wait()
    got2 = ids2_recv[0]
    for k in range(1, N_Y):
        got2 = got2 + ids2_recv[k]
    in_block = iota((1, D), 1) % 32
    norm = BATCH / jnp.sum(jnp.where(in_block == 24, got2, 0.0), axis=1, keepdims=True)
    row_ids = jnp.where(in_block < 2 * N_Z, got2, 0.0).astype(jnp.int32)

    member[...] = jnp.where(iota((ROWS_DEV, D), 0) + 1 == row_ids, 1.0, 0.0).astype(jnp.bfloat16)
    query_grad = dq_keep[0] + dq_got[0]
    for k in (1, 3, 2):
        chip_copy(k).wait_recv()
        query_grad = query_grad + dq_in[k].astype(jnp.float32)
    dq_ref[...] = (query_grad * norm).astype(jnp.bfloat16)


    for copy in sent:
        copy.wait_send()
    for k in range(N_X):
        pair_copy(k).wait_send()
    for k in range(1, N_X):
        chip_copy(k).wait_send()
    for j in range(N_GRP - 1):
        stats_copy(j).wait_send()
    pltpu.make_async_copy(ids1_send.at[pl.ds(0, N_Z - 1)], ids1_send.at[pl.ds(0, N_Z - 1)], i1_send_sem).wait()
    pltpu.make_async_copy(ids2_send.at[pl.ds(0, N_Y - 1)], ids2_send.at[pl.ds(0, N_Y - 1)], i2_send_sem).wait()
    pltpu.make_async_copy(send1.at[pl.ds(0, N_Z - 1)], send1.at[pl.ds(0, N_Z - 1)], r1_send_sem).wait()
    pltpu.make_async_copy(recv2.at[pl.ds(0, N_Y - 1)], recv2.at[pl.ds(0, N_Y - 1)], r2_recv_sem).wait()
    tab_ref[...] = norm * jnp.dot(
        member[...], recv2[...].reshape(N_Y * 32, D), preferred_element_type=jnp.float32
    )
    pltpu.make_async_copy(send2.at[pl.ds(0, N_Y - 1)], send2.at[pl.ds(0, N_Y - 1)], r2_send_sem).wait()


def shards(queries, item_vecs, log_q, weights, item_owner, item_row):
    vmem = pl.BlockSpec(memory_space=pltpu.VMEM)
    bf16, f32 = jnp.bfloat16, jnp.float32
    dma = pltpu.SemaphoreType.DMA
    return pl.pallas_call(
        kernel,
        out_shape=(
            jax.ShapeDtypeStruct((B_DEV, D), bf16),
            jax.ShapeDtypeStruct((ROWS_DEV, D), f32),
        ),
        in_specs=[pl.BlockSpec(memory_space=pltpu.HBM)] * 6,
        out_specs=(vmem, vmem),
        scratch_shapes=[
            pltpu.VMEM((PER_ITEM,), bf16),
            pltpu.VMEM((B_DEV,), bf16),
            pltpu.VMEM((1, PER_ITEM), jnp.int32),
            pltpu.VMEM((1, PER_ITEM), jnp.int32),
            pltpu.VMEM((PER_ITEM, D), bf16),
            pltpu.VMEM((N_GRP, Q_ROWS, D), bf16),
            pltpu.VMEM((N_GRP, PER_ITEM, B_DEV), f32),
            pltpu.VMEM((PER_ITEM, N_GRP * B_DEV), bf16),
            pltpu.VMEM((N_GRP, 1, 256), f32),
            pltpu.VMEM((N_GRP, N_GRP, 256), f32),
            pltpu.VMEM((N_X, B_DEV, D), f32),
            pltpu.VMEM((N_X, B_DEV, D), f32),
            pltpu.VMEM((N_X, B_DEV, D), f32),
            pltpu.VMEM((N_X, B_DEV, D), bf16),
            pltpu.VMEM((N_X, B_DEV, D), bf16),
            pltpu.VMEM((N_Z, 1, 128), f32),
            pltpu.VMEM((N_Z, 1, 128), f32),
            pltpu.VMEM((16, 128), f32),
            pltpu.VMEM((N_Y, 1, D), f32),
            pltpu.VMEM((N_Y, 1, D), f32),
            pltpu.VMEM((2 * N_Z * N_Y, PER_ITEM), bf16),
            pltpu.VMEM((N_Y * 32, 2 * N_Z * N_Y), bf16),
            pltpu.VMEM((ROWS_DEV, D), bf16),
            pltpu.VMEM((N_Z, 2 * N_Y, D), bf16),
            pltpu.VMEM((N_Z, 2 * N_Y, D), bf16),
            pltpu.VMEM((N_Y, 32, D), bf16),
            pltpu.VMEM((N_Y, 32, D), bf16),
            dma((6,)), pltpu.SemaphoreType.REGULAR((3,)), pltpu.SemaphoreType.REGULAR((2,)),
            dma((7,)), dma((N_GRP,)),
            dma((N_GRP,)), dma((N_GRP,)),
            dma((N_X,)), dma((N_X,)), dma((N_X,)), dma((N_X,)),
            dma, dma, dma, dma, dma, dma, dma, dma,
        ],
        compiler_params=pltpu.CompilerParams(
            collective_id=0, has_side_effects=True, vmem_limit_bytes=32 * 1024 * 1024
        ),
    )(*(
        pltpu.with_memory_space_constraint(operand, pltpu.HBM)
        for operand in (
            queries,
            item_vecs,
            log_q,
            weights,
            item_owner.reshape(1, PER_ITEM),
            item_row.reshape(1, PER_ITEM),
        )
    ))


def solution(mesh):
    in_specs = (
        P(("grp", "dp"), None),
        P(("grp", "dp"), None),
        P(("grp", "dp")),
        P(("grp", "dp")),
        P(("grp", "dp"), None),
        P(("grp", "dp")),
    )
    out_specs = (P(("grp", "dp"), None), P(("grp", "dp"), None))
    return jax.shard_map(shards, mesh=mesh, in_specs=in_specs, out_specs=out_specs, check_vma=False)
```

```python
import functools

import jax
import jax.numpy as jnp
from jax import lax
from jax.experimental import pallas as pl
from jax.experimental.pallas import tpu as pltpu
from jax.sharding import PartitionSpec as P

N_X = 4
N_GRP = 8
N_Z = 12
N_Y = 8
B_DEV = 128
Q_ROWS = 144
PER_ITEM = 160
ROWS_DEV = 1024
D = 256
BATCH = 98304
CHUNKS = 4
Z_ORDER = (6, 5, 7, 4, 8, 3, 9, 2, 10, 1, 11)
Y_ORDER = (4, 3, 5, 2, 6, 1, 7)
MESH = pl.DeviceIdType.MESH
HIGHEST = lax.Precision.HIGHEST


def nt_dot(left, right, precision=None):
    return lax.dot_general(
        left, right, (((1,), (1,)), ((), ())), precision=precision, preferred_element_type=jnp.float32
    )


def tn_dot(left, right):
    return lax.dot_general(left, right, (((0,), (0,)), ((), ())), preferred_element_type=jnp.float32)


def iota(shape, dim):
    return lax.broadcasted_iota(jnp.int32, shape, dim)


def kernel(
    q_hbm, it_hbm, lq_hbm, w_hbm, own_hbm, row_hbm,
    dq_ref, rows_ref, member, norm_ref,
    lq_ref, w_ref, own_ref, row_ref,
    items, q_all, cross, grads, own_stats, stats, dq_keep, dq_send, dq_got, dq_terms, dq_in,
    ids1_send, ids1_recv, ids1_flat, ids2_send, ids2_recv,
    slots, perm, send1, recv1, send2, recv2,
    in_sem, z_sems, y_sems,
    q_send_sem, q_recv_sem, st_send_sem, st_recv_sem,
    dp_send_sem, dp_recv_sem, dx_send_sem, dx_recv_sem,
    i1_send_sem, i1_recv_sem, i2_send_sem, i2_recv_sem,
    r1_send_sem, r1_recv_sem, r2_send_sem, r2_recv_sem,
):
    g = lax.axis_index("grp")
    d = lax.axis_index("dp")
    z, y = d // N_Y, d % N_Y
    x, c = g // 2, g % 2
    sib = 2 * x + 1 - c
    ahead = 1 - 2 * c

    loads = [
        pltpu.make_async_copy(src, dst, in_sem.at[i])
        for i, (src, dst) in enumerate((
            (it_hbm, items),
            (q_hbm, q_all.at[g, pl.ds(0, B_DEV)]),
            (lq_hbm, lq_ref),
            (w_hbm, w_ref),
            (own_hbm, own_ref),
            (row_hbm, row_ref),
        ))
    ]
    for load in loads:
        load.start()

    barrier = pltpu.get_barrier_semaphore()

    def chip(dx):
        return (x + dx + N_X) % N_X

    behind_x, ahead_x, far_x = chip(-ahead), chip(ahead), chip(2)
    behind_g, ahead_g, far_g = 2 * behind_x + c, 2 * ahead_x + c, 2 * far_x + c
    for peer in (ahead_g, behind_g, sib, far_g):
        pl.semaphore_signal(barrier, inc=1, device_id={"grp": peer}, device_id_type=MESH)

    def z_peer(step):
        return {"dp": ((z + step + N_Z) % N_Z) * N_Y + y}

    def y_peer(step):
        return {"dp": z * N_Y + (y + step + N_Y) % N_Y}

    def signal_pair(sem, peer, step):
        pl.semaphore_signal(sem, inc=1, device_id=peer(step), device_id_type=MESH)
        pl.semaphore_signal(sem, inc=1, device_id=peer(-step), device_id_type=MESH)

    signal_pair(barrier, z_peer, 1)
    signal_pair(barrier, y_peer, 1)

    for load in loads:
        load.wait()
    log_q = lq_ref[...].astype(jnp.float32).reshape(1, PER_ITEM)
    weights = w_ref[...].astype(jnp.float32).reshape(1, B_DEV)
    padded_w = jnp.concatenate([weights, jnp.zeros((1, D - B_DEV), jnp.float32)], axis=1)
    q_all[g, B_DEV:Q_ROWS, :] = jnp.broadcast_to(padded_w, (Q_ROWS - B_DEV, D)).astype(jnp.bfloat16)

    pl.semaphore_wait(barrier, 4 + 2 + 2)

    def block_copy(buf, block, target, send_sem, recv_sem, index):
        return pltpu.make_async_remote_copy(
            src_ref=buf.at[block],
            dst_ref=buf.at[block],
            send_sem=send_sem.at[index],
            recv_sem=recv_sem.at[block],
            device_id={"grp": target},
            device_id_type=MESH,
        )

    sent = []

    def send(buf, block, target, sems, index):
        copy = block_copy(buf, block, target, sems[0], sems[1], index)
        copy.start()
        sent.append(copy)

    def arrived(buf, block, sems):
        block_copy(buf, block, sib, sems[0], sems[1], 0).wait_recv()

    q_sems = (q_send_sem, q_recv_sem)

    def first_sends(buf, sems):
        send(buf, g, far_g, sems, 3)
        send(buf, g, ahead_g, sems, 0)
        send(buf, g, behind_g, sems, 1)
        send(buf, g, sib, sems, 2)

    first_sends(q_all, q_sems)

    signal_pair(z_sems.at[0], z_peer, 1)
    signal_pair(y_sems.at[0], y_peer, 1)

    owner_i = own_ref[...]
    row_i = row_ref[...]

    owner = owner_i.astype(jnp.float32)
    sub, lane = iota((PER_ITEM, PER_ITEM), 0), iota((PER_ITEM, PER_ITEM), 1)
    eye = sub == lane
    owner_col = jnp.sum(jnp.where(eye, owner, 0.0), axis=1, keepdims=True)
    lq_col = jnp.sum(jnp.where(eye, log_q, 0.0), axis=1, keepdims=True)
    same = jnp.where((owner_col == owner) & (sub < lane), 1.0, 0.0)
    place = jnp.sum(same, axis=0, keepdims=True).astype(jnp.int32)
    dest_z = owner_i // N_Y
    slot = owner_i * 2 + place
    slot_z = slot - dest_z * (2 * N_Y)

    kind = iota((48, PER_ITEM), 0) // 16
    sub48 = iota((48, PER_ITEM), 0) % 16
    part = jnp.where(kind == 0, row_i // 32, jnp.where(kind == 1, row_i % 32, 1)).astype(jnp.float32)
    left = jnp.where(sub48 == dest_z, part, 0.0).astype(jnp.bfloat16)
    right = jnp.where(iota((128, PER_ITEM), 0) == slot_z, 1.0, 0.0).astype(jnp.bfloat16)
    found = nt_dot(left, right)
    ids1 = found[0:16] * 32.0 + found[16:32] + found[32:48]

    slots[...] = jnp.where(iota((2 * N_Z * N_Y, PER_ITEM), 0) == slot, 1.0, 0.0).astype(jnp.bfloat16)
    pr, pc = iota((N_Y * 32, 2 * N_Z * N_Y), 0), iota((N_Y * 32, 2 * N_Z * N_Y), 1)
    in_y = pr % 32
    perm[...] = jnp.where(
        (in_y < 2 * N_Z) & (pc == (in_y // 2) * (2 * N_Y) + (pr // 32) * 2 + in_y % 2), 1.0, 0.0
    ).astype(jnp.bfloat16)

    def block_logits(block):
        value = nt_dot(items[...], q_all[block, 0:B_DEV, :]) - lq_col
        top = jnp.max(value, axis=0, keepdims=True)
        shifted = jnp.exp(value - top)
        cross[block] = shifted
        own_stats[block, :, 0:128] = top
        own_stats[block, :, 128:256] = jnp.sum(shifted, axis=0, keepdims=True)

    def other_core(chip_x):
        return 2 * chip_x + 1 - c

    block_logits(g)
    arrived(q_all, sib, q_sems)
    block_logits(sib)
    arrived(q_all, behind_g, q_sems)
    send(q_all, behind_g, sib, q_sems, 4)
    arrived(q_all, ahead_g, q_sems)
    send(q_all, ahead_g, sib, q_sems, 5)
    pl.semaphore_wait(z_sems.at[0], 2)
    signal_pair(z_sems.at[1], z_peer, 2)
    pl.semaphore_wait(y_sems.at[0], 2)
    signal_pair(y_sems.at[1], y_peer, 2)
    block_logits(behind_g)
    block_logits(ahead_g)
    arrived(q_all, far_g, q_sems)
    send(q_all, far_g, sib, q_sems, 6)
    arrived(q_all, other_core(behind_x), q_sems)
    block_logits(other_core(behind_x))
    arrived(q_all, other_core(ahead_x), q_sems)
    block_logits(other_core(ahead_x))
    block_logits(far_g)
    pl.semaphore_wait(z_sems.at[1], 2)
    signal_pair(z_sems.at[2], z_peer, 2)
    arrived(q_all, other_core(far_x), q_sems)
    block_logits(other_core(far_x))

    for b in range(N_GRP):
        stats[g, b : b + 1, :] = own_stats[b]

    others = (
        far_g, other_core(far_x), ahead_g, behind_g, other_core(ahead_x), other_core(behind_x), sib
    )

    def stats_copy(j):
        return block_copy(stats, g, others[j], st_send_sem, st_recv_sem, j)

    for j in range(N_GRP - 1):
        stats_copy(j).start()

    block_weights = [q_all[b, B_DEV:Q_ROWS, 0:B_DEV].astype(jnp.float32)[0:1] for b in range(N_GRP)]
    all_weights = block_weights[0]
    for b in range(1, N_GRP):
        all_weights = all_weights + block_weights[b]
    group_sum = jnp.sum(all_weights, axis=1, keepdims=True)
    ids1 = jnp.where(iota((16, 128), 1) == 2 * N_Y, group_sum, ids1)
    for k in range(N_Z):
        ids1_send[k] = ids1[k : k + 1]
    ids1_recv[z] = ids1_send[z]

    pl.semaphore_wait(y_sems.at[1], 2)
    pl.semaphore_wait(z_sems.at[2], 2)

    def ids1_copy(j):
        zt = jnp.where(z + j >= N_Z, z + j - N_Z, z + j)
        return pltpu.make_async_remote_copy(
            src_ref=ids1_send.at[zt],
            dst_ref=ids1_recv.at[z],
            send_sem=i1_send_sem,
            recv_sem=i1_recv_sem,
            device_id={"dp": zt * N_Y + y},
            device_id_type=MESH,
        )

    for j in Z_ORDER:
        ids1_copy(j).start()

    for other in others:
        block_copy(stats, other, sib, st_send_sem, st_recv_sem, 0).wait_recv()

    tops = [stats[b, :, 0:128] for b in range(N_GRP)]
    top = functools.reduce(jnp.maximum, tops)
    total = jnp.zeros((N_GRP, B_DEV), jnp.float32)
    for b in range(N_GRP):
        total = total + jnp.exp(tops[b] - top) * stats[b, :, 128:256]
    scale = jnp.exp(stats[g, :, 0:128] - top) / total
    pos_sub, pos_lane = iota((PER_ITEM, B_DEV), 0), iota((PER_ITEM, B_DEV), 1)
    for b in range(N_GRP):
        share = cross[b] * scale[b : b + 1]
        share = share - jnp.where(pos_sub + b * PER_ITEM == pos_lane + g * PER_ITEM, 1.0, 0.0)
        grads[:, b * B_DEV : (b + 1) * B_DEV] = (block_weights[b] * share).astype(jnp.bfloat16)
    item_grad = jnp.dot(
        grads[...], q_all[:, 0:B_DEV, :].reshape(N_GRP * B_DEV, D), preferred_element_type=jnp.float32
    ).astype(jnp.bfloat16)
    placed = jnp.dot(slots[...], item_grad, preferred_element_type=jnp.float32)
    send1[...] = placed.astype(jnp.bfloat16).reshape(N_Z, 2 * N_Y, D)

    def rows1_copy(j):
        zt = jnp.where(z + j >= N_Z, z + j - N_Z, z + j)
        return pltpu.make_async_remote_copy(
            src_ref=send1.at[zt],
            dst_ref=recv1.at[z],
            send_sem=r1_send_sem,
            recv_sem=r1_recv_sem,
            device_id={"dp": zt * N_Y + y},
            device_id_type=MESH,
        )

    for j in Z_ORDER:
        rows1_copy(j).start()
    recv1[z] = send1[z]

    def query_term(block):
        columns = pl.ds(pl.multiple_of(block * B_DEV, B_DEV), B_DEV)
        return tn_dot(grads[:, columns], items[...])

    def pair_copy(k):
        return pltpu.make_async_remote_copy(
            src_ref=dq_send.at[k],
            dst_ref=dq_got.at[k],
            send_sem=dp_send_sem.at[k],
            recv_sem=dp_recv_sem.at[k],
            device_id={"grp": sib},
            device_id_type=MESH,
        )

    for k in range(N_X):
        dq_send[k] = query_term(2 * chip(k) + 1 - c)
        pair_copy(k).start()
    for k in range(N_X):
        dq_keep[k] = query_term(2 * chip(k) + c)

    pltpu.make_async_copy(ids1_recv.at[pl.ds(0, N_Z - 1)], ids1_recv.at[pl.ds(0, N_Z - 1)], i1_recv_sem).wait()
    ids1_flat[...] = jnp.zeros((16, 128), jnp.float32)
    for k in range(N_Z):
        ids1_flat[k : k + 1, :] = ids1_recv[k]
    got1 = ids1_flat[...]
    y_sub, l_lane = iota((N_Y, 128), 0), iota((N_Y, 128), 1)
    z_sub, s_lane = iota((16, D), 0), iota((16, D), 1)
    ids2 = jnp.zeros((N_Y, D), jnp.float32)
    for k in range(2):
        pick = jnp.where(l_lane == 2 * y_sub + k, 1.0, 0.0)
        spread = jnp.where(s_lane == y * 32 + 2 * z_sub + k, 1.0, 0.0)
        picked = nt_dot(pick, got1, HIGHEST)
        ids2 = ids2 + jnp.dot(picked, spread, precision=HIGHEST, preferred_element_type=jnp.float32)
    summed = jnp.sum(got1, axis=0, keepdims=True)
    w_z = jnp.sum(jnp.where(iota((1, 128), 1) == 2 * N_Y, summed, 0.0), axis=1, keepdims=True)
    ids2 = jnp.where(iota((N_Y, D), 1) == y * 32 + 24, w_z, ids2)
    for k in range(N_Y):
        ids2_send[k] = ids2[k : k + 1]
    ids2_recv[y] = ids2_send[y]

    def ids2_copy(j):
        yt = jnp.where(y + j >= N_Y, y + j - N_Y, y + j)
        return pltpu.make_async_remote_copy(
            src_ref=ids2_send.at[yt],
            dst_ref=ids2_recv.at[y],
            send_sem=i2_send_sem,
            recv_sem=i2_recv_sem,
            device_id={"dp": z * N_Y + yt},
            device_id_type=MESH,
        )

    for j in Y_ORDER:
        ids2_copy(j).start()

    def chip_copy(k):
        return pltpu.make_async_remote_copy(
            src_ref=dq_terms.at[k],
            dst_ref=dq_in.at[k],
            send_sem=dx_send_sem.at[k],
            recv_sem=dx_recv_sem.at[k],
            device_id={"grp": 2 * chip(k) + c},
            device_id_type=MESH,
        )

    for k in (2, 1, 3):
        pair_copy(k).wait_recv()
        dq_terms[k] = (dq_keep[k] + dq_got[k]).astype(jnp.bfloat16)
        chip_copy(k).start()
    pair_copy(0).wait_recv()

    pltpu.make_async_copy(recv1.at[pl.ds(0, N_Z - 1)], recv1.at[pl.ds(0, N_Z - 1)], r1_recv_sem).wait()
    turned = jnp.dot(perm[...], recv1[...].reshape(2 * N_Z * N_Y, D), preferred_element_type=jnp.float32)
    send2[...] = turned.astype(jnp.bfloat16).reshape(N_Y, 32, D)

    def rows2_copy(j):
        yt = jnp.where(y + j >= N_Y, y + j - N_Y, y + j)
        return pltpu.make_async_remote_copy(
            src_ref=send2.at[yt],
            dst_ref=recv2.at[y],
            send_sem=r2_send_sem,
            recv_sem=r2_recv_sem,
            device_id={"dp": z * N_Y + yt},
            device_id_type=MESH,
        )

    for j in Y_ORDER:
        rows2_copy(j).start()
    recv2[y] = send2[y]

    pltpu.make_async_copy(ids2_recv.at[pl.ds(0, N_Y - 1)], ids2_recv.at[pl.ds(0, N_Y - 1)], i2_recv_sem).wait()
    got2 = ids2_recv[0]
    for k in range(1, N_Y):
        got2 = got2 + ids2_recv[k]
    in_block = iota((1, D), 1) % 32
    norm = BATCH / jnp.sum(jnp.where(in_block == 24, got2, 0.0), axis=1, keepdims=True)
    row_ids = jnp.where(in_block < 2 * N_Z, got2, 0.0).astype(jnp.int32)

    member[...] = jnp.where(iota((ROWS_DEV, D), 0) + 1 == row_ids, 1.0, 0.0).astype(jnp.bfloat16)
    query_grad = dq_keep[0] + dq_got[0]
    for k in (1, 3, 2):
        chip_copy(k).wait_recv()
        query_grad = query_grad + dq_in[k].astype(jnp.float32)
    dq_ref[...] = (query_grad * norm).astype(jnp.bfloat16)


    for copy in sent:
        copy.wait_send()
    for k in range(N_X):
        pair_copy(k).wait_send()
    for k in range(1, N_X):
        chip_copy(k).wait_send()
    for j in range(N_GRP - 1):
        stats_copy(j).wait_send()
    pltpu.make_async_copy(ids1_send.at[pl.ds(0, N_Z - 1)], ids1_send.at[pl.ds(0, N_Z - 1)], i1_send_sem).wait()
    pltpu.make_async_copy(ids2_send.at[pl.ds(0, N_Y - 1)], ids2_send.at[pl.ds(0, N_Y - 1)], i2_send_sem).wait()
    pltpu.make_async_copy(send1.at[pl.ds(0, N_Z - 1)], send1.at[pl.ds(0, N_Z - 1)], r1_send_sem).wait()
    pltpu.make_async_copy(recv2.at[pl.ds(0, N_Y - 1)], recv2.at[pl.ds(0, N_Y - 1)], r2_recv_sem).wait()
    rows_ref[...] = recv2[...].reshape(N_Y * 32, D)
    norm_ref[...] = jnp.broadcast_to(norm, (1, D))
    pltpu.make_async_copy(send2.at[pl.ds(0, N_Y - 1)], send2.at[pl.ds(0, N_Y - 1)], r2_send_sem).wait()


def write_out(query_ref, rows_ref, member_ref, norm_ref, dq_out, tab_out, table, dq_sem, tab_sems):
    query_copy = pltpu.make_async_copy(query_ref, dq_out, dq_sem)
    query_copy.start()
    size = ROWS_DEV // CHUNKS
    copies = []
    for k in range(CHUNKS):
        part = slice(k * size, (k + 1) * size)
        table[part, :] = norm_ref[...] * jnp.dot(
            member_ref[part, :], rows_ref[...], preferred_element_type=jnp.float32
        )
        copy = pltpu.make_async_copy(
            table.at[pl.ds(k * size, size)], tab_out.at[pl.ds(k * size, size)], tab_sems.at[k]
        )
        copy.start()
        copies.append(copy)
    query_copy.wait()
    for copy in copies:
        copy.wait()


def shards(queries, item_vecs, log_q, weights, item_owner, item_row):
    vmem = pl.BlockSpec(memory_space=pltpu.VMEM)
    bf16, f32 = jnp.bfloat16, jnp.float32
    dma = pltpu.SemaphoreType.DMA
    query_grad, rows, member, norm = pl.pallas_call(
        kernel,
        out_shape=(
            jax.ShapeDtypeStruct((B_DEV, D), bf16),
            jax.ShapeDtypeStruct((N_Y * 32, D), bf16),
            jax.ShapeDtypeStruct((ROWS_DEV, D), bf16),
            jax.ShapeDtypeStruct((1, D), f32),
        ),
        in_specs=[pl.BlockSpec(memory_space=pltpu.HBM)] * 6,
        out_specs=(vmem,) * 4,
        scratch_shapes=[
            pltpu.VMEM((PER_ITEM,), bf16),
            pltpu.VMEM((B_DEV,), bf16),
            pltpu.VMEM((1, PER_ITEM), jnp.int32),
            pltpu.VMEM((1, PER_ITEM), jnp.int32),
            pltpu.VMEM((PER_ITEM, D), bf16),
            pltpu.VMEM((N_GRP, Q_ROWS, D), bf16),
            pltpu.VMEM((N_GRP, PER_ITEM, B_DEV), f32),
            pltpu.VMEM((PER_ITEM, N_GRP * B_DEV), bf16),
            pltpu.VMEM((N_GRP, 1, 256), f32),
            pltpu.VMEM((N_GRP, N_GRP, 256), f32),
            pltpu.VMEM((N_X, B_DEV, D), f32),
            pltpu.VMEM((N_X, B_DEV, D), f32),
            pltpu.VMEM((N_X, B_DEV, D), f32),
            pltpu.VMEM((N_X, B_DEV, D), bf16),
            pltpu.VMEM((N_X, B_DEV, D), bf16),
            pltpu.VMEM((N_Z, 1, 128), f32),
            pltpu.VMEM((N_Z, 1, 128), f32),
            pltpu.VMEM((16, 128), f32),
            pltpu.VMEM((N_Y, 1, D), f32),
            pltpu.VMEM((N_Y, 1, D), f32),
            pltpu.VMEM((2 * N_Z * N_Y, PER_ITEM), bf16),
            pltpu.VMEM((N_Y * 32, 2 * N_Z * N_Y), bf16),
            pltpu.VMEM((N_Z, 2 * N_Y, D), bf16),
            pltpu.VMEM((N_Z, 2 * N_Y, D), bf16),
            pltpu.VMEM((N_Y, 32, D), bf16),
            pltpu.VMEM((N_Y, 32, D), bf16),
            dma((6,)), pltpu.SemaphoreType.REGULAR((3,)), pltpu.SemaphoreType.REGULAR((2,)),
            dma((7,)), dma((N_GRP,)),
            dma((N_GRP,)), dma((N_GRP,)),
            dma((N_X,)), dma((N_X,)), dma((N_X,)), dma((N_X,)),
            dma, dma, dma, dma, dma, dma, dma, dma,
        ],
        compiler_params=pltpu.CompilerParams(
            collective_id=0, has_side_effects=True, vmem_limit_bytes=32 * 1024 * 1024
        ),
    )(*(
        pltpu.with_memory_space_constraint(operand, pltpu.HBM)
        for operand in (
            queries,
            item_vecs,
            log_q,
            weights,
            item_owner.reshape(1, PER_ITEM),
            item_row.reshape(1, PER_ITEM),
        )
    ))
    hbm = pl.BlockSpec(memory_space=pl.ANY)
    return pl.pallas_call(
        write_out,
        out_shape=(
            jax.ShapeDtypeStruct((B_DEV, D), bf16),
            jax.ShapeDtypeStruct((ROWS_DEV, D), f32),
        ),
        in_specs=[vmem] * 4,
        out_specs=(hbm, hbm),
        scratch_shapes=[pltpu.VMEM((ROWS_DEV, D), f32), dma, dma((CHUNKS,))],
        compiler_params=pltpu.CompilerParams(vmem_limit_bytes=32 * 1024 * 1024),
    )(query_grad, rows, member, norm)


def solution(mesh):
    in_specs = (
        P(("grp", "dp"), None),
        P(("grp", "dp"), None),
        P(("grp", "dp")),
        P(("grp", "dp")),
        P(("grp", "dp"), None),
        P(("grp", "dp")),
    )
    out_specs = (P(("grp", "dp"), None), P(("grp", "dp"), None))
    return jax.shard_map(shards, mesh=mesh, in_specs=in_specs, out_specs=out_specs, check_vma=False)
```

```python
import functools

import jax
import jax.numpy as jnp
from jax import lax
from jax.experimental import pallas as pl
from jax.experimental.pallas import tpu as pltpu
from jax.sharding import PartitionSpec as P

N_X = 4
N_GRP = 8
N_Z = 12
N_Y = 8
B_DEV = 128
Q_ROWS = 144
PER_ITEM = 160
ROWS_DEV = 1024
D = 256
BATCH = 98304
CHUNKS = 4
Z_ORDER = (6, 5, 7, 4, 8, 3, 9, 2, 10, 1, 11)
Y_ORDER = (4, 3, 5, 2, 6, 1, 7)
MESH = pl.DeviceIdType.MESH
HIGHEST = lax.Precision.HIGHEST


def nt_dot(left, right, precision=None):
    return lax.dot_general(
        left, right, (((1,), (1,)), ((), ())), precision=precision, preferred_element_type=jnp.float32
    )


def tn_dot(left, right):
    return lax.dot_general(left, right, (((0,), (0,)), ((), ())), preferred_element_type=jnp.float32)


def iota(shape, dim):
    return lax.broadcasted_iota(jnp.int32, shape, dim)


def kernel(
    q_hbm, it_hbm, lq_hbm, w_hbm, own_hbm, row_hbm,
    dq_ref, rows_ref, member, norm_ref,
    lq_ref, w_ref, own_ref, row_ref,
    items, q_all, cross, grads, own_stats, stats, dq_keep, dq_send, dq_got, dq_terms, dq_in,
    ids1_send, ids1_recv, ids1_flat, ids2_send, ids2_recv,
    slots, perm, send1, recv1, send2, recv2,
    in_sem, z_sems, y_sem,
    q_send_sem, q_recv_sem, st_send_sem, st_recv_sem,
    dp_send_sem, dp_recv_sem, dx_send_sem, dx_recv_sem,
    i1_send_sem, i1_recv_sem, i2_send_sem, i2_recv_sem,
    r1_send_sem, r1_recv_sem, r2_send_sem, r2_recv_sem,
):
    g = lax.axis_index("grp")
    d = lax.axis_index("dp")
    z, y = d // N_Y, d % N_Y
    x, c = g // 2, g % 2
    sib = 2 * x + 1 - c
    ahead = 1 - 2 * c

    loads = [
        pltpu.make_async_copy(src, dst, in_sem.at[i])
        for i, (src, dst) in enumerate((
            (it_hbm, items),
            (q_hbm, q_all.at[g, pl.ds(0, B_DEV)]),
            (lq_hbm, lq_ref),
            (w_hbm, w_ref),
            (own_hbm, own_ref),
            (row_hbm, row_ref),
        ))
    ]
    for load in loads:
        load.start()

    barrier = pltpu.get_barrier_semaphore()

    def chip(dx):
        return (x + dx + N_X) % N_X

    behind_x, ahead_x, far_x = chip(-ahead), chip(ahead), chip(2)
    behind_g, ahead_g, far_g = 2 * behind_x + c, 2 * ahead_x + c, 2 * far_x + c
    for peer in (ahead_g, behind_g, sib, far_g):
        pl.semaphore_signal(barrier, inc=1, device_id={"grp": peer}, device_id_type=MESH)

    def z_peer(step):
        return {"dp": ((z + step + N_Z) % N_Z) * N_Y + y}

    def y_peer(step):
        return {"dp": z * N_Y + (y + step + N_Y) % N_Y}

    def signal_pair(sem, peer, step):
        pl.semaphore_signal(sem, inc=1, device_id=peer(step), device_id_type=MESH)
        pl.semaphore_signal(sem, inc=1, device_id=peer(-step), device_id_type=MESH)

    for step in (2, 1):
        signal_pair(barrier, z_peer, step)
        signal_pair(barrier, y_peer, step)

    for load in loads:
        load.wait()
    log_q = lq_ref[...].astype(jnp.float32).reshape(1, PER_ITEM)
    weights = w_ref[...].astype(jnp.float32).reshape(1, B_DEV)
    padded_w = jnp.concatenate([weights, jnp.zeros((1, D - B_DEV), jnp.float32)], axis=1)
    q_all[g, B_DEV:Q_ROWS, :] = jnp.broadcast_to(padded_w, (Q_ROWS - B_DEV, D)).astype(jnp.bfloat16)

    pl.semaphore_wait(barrier, 4 + 4 + 4)

    def block_copy(buf, block, target, send_sem, recv_sem, index):
        return pltpu.make_async_remote_copy(
            src_ref=buf.at[block],
            dst_ref=buf.at[block],
            send_sem=send_sem.at[index],
            recv_sem=recv_sem.at[block],
            device_id={"grp": target},
            device_id_type=MESH,
        )

    sent = []

    def send(buf, block, target, sems, index):
        copy = block_copy(buf, block, target, sems[0], sems[1], index)
        copy.start()
        sent.append(copy)

    def arrived(buf, block, sems):
        block_copy(buf, block, sib, sems[0], sems[1], 0).wait_recv()

    q_sems = (q_send_sem, q_recv_sem)

    def first_sends(buf, sems):
        send(buf, g, far_g, sems, 3)
        send(buf, g, ahead_g, sems, 0)
        send(buf, g, behind_g, sems, 1)
        send(buf, g, sib, sems, 2)

    first_sends(q_all, q_sems)

    signal_pair(z_sems.at[0], z_peer, 2)
    signal_pair(y_sem, y_peer, 2)

    owner_i = own_ref[...]
    row_i = row_ref[...]

    owner = owner_i.astype(jnp.float32)
    sub, lane = iota((PER_ITEM, PER_ITEM), 0), iota((PER_ITEM, PER_ITEM), 1)
    eye = sub == lane
    owner_col = jnp.sum(jnp.where(eye, owner, 0.0), axis=1, keepdims=True)
    lq_col = jnp.sum(jnp.where(eye, log_q, 0.0), axis=1, keepdims=True)
    same = jnp.where((owner_col == owner) & (sub < lane), 1.0, 0.0)
    place = jnp.sum(same, axis=0, keepdims=True).astype(jnp.int32)
    dest_z = owner_i // N_Y
    slot = owner_i * 2 + place
    slot_z = slot - dest_z * (2 * N_Y)

    kind = iota((48, PER_ITEM), 0) // 16
    sub48 = iota((48, PER_ITEM), 0) % 16
    part = jnp.where(kind == 0, row_i // 32, jnp.where(kind == 1, row_i % 32, 1)).astype(jnp.float32)
    left = jnp.where(sub48 == dest_z, part, 0.0).astype(jnp.bfloat16)
    right = jnp.where(iota((128, PER_ITEM), 0) == slot_z, 1.0, 0.0).astype(jnp.bfloat16)
    found = nt_dot(left, right)
    ids1 = found[0:16] * 32.0 + found[16:32] + found[32:48]

    slots[...] = jnp.where(iota((2 * N_Z * N_Y, PER_ITEM), 0) == slot, 1.0, 0.0).astype(jnp.bfloat16)
    pr, pc = iota((N_Y * 32, 2 * N_Z * N_Y), 0), iota((N_Y * 32, 2 * N_Z * N_Y), 1)
    in_y = pr % 32
    perm[...] = jnp.where(
        (in_y < 2 * N_Z) & (pc == (in_y // 2) * (2 * N_Y) + (pr // 32) * 2 + in_y % 2), 1.0, 0.0
    ).astype(jnp.bfloat16)

    def block_logits(block):
        value = nt_dot(items[...], q_all[block, 0:B_DEV, :]) - lq_col
        top = jnp.max(value, axis=0, keepdims=True)
        shifted = jnp.exp(value - top)
        cross[block] = shifted
        own_stats[block, :, 0:128] = top
        own_stats[block, :, 128:256] = jnp.sum(shifted, axis=0, keepdims=True)

    def other_core(chip_x):
        return 2 * chip_x + 1 - c

    block_logits(g)
    arrived(q_all, sib, q_sems)
    block_logits(sib)
    arrived(q_all, behind_g, q_sems)
    send(q_all, behind_g, sib, q_sems, 4)
    arrived(q_all, ahead_g, q_sems)
    send(q_all, ahead_g, sib, q_sems, 5)
    pl.semaphore_wait(z_sems.at[0], 2)
    signal_pair(z_sems.at[1], z_peer, 2)
    block_logits(behind_g)
    block_logits(ahead_g)
    arrived(q_all, far_g, q_sems)
    send(q_all, far_g, sib, q_sems, 6)
    arrived(q_all, other_core(behind_x), q_sems)
    block_logits(other_core(behind_x))
    arrived(q_all, other_core(ahead_x), q_sems)
    block_logits(other_core(ahead_x))
    block_logits(far_g)
    arrived(q_all, other_core(far_x), q_sems)
    block_logits(other_core(far_x))

    for b in range(N_GRP):
        stats[g, b : b + 1, :] = own_stats[b]

    others = (
        far_g, other_core(far_x), ahead_g, behind_g, other_core(ahead_x), other_core(behind_x), sib
    )

    def stats_copy(j):
        return block_copy(stats, g, others[j], st_send_sem, st_recv_sem, j)

    for j in range(N_GRP - 1):
        stats_copy(j).start()

    block_weights = [q_all[b, B_DEV:Q_ROWS, 0:B_DEV].astype(jnp.float32)[0:1] for b in range(N_GRP)]
    all_weights = block_weights[0]
    for b in range(1, N_GRP):
        all_weights = all_weights + block_weights[b]
    group_sum = jnp.sum(all_weights, axis=1, keepdims=True)
    ids1 = jnp.where(iota((16, 128), 1) == 2 * N_Y, group_sum, ids1)
    for k in range(N_Z):
        ids1_send[k] = ids1[k : k + 1]
    ids1_recv[z] = ids1_send[z]

    pl.semaphore_wait(y_sem, 2)
    pl.semaphore_wait(z_sems.at[1], 2)

    def ids1_copy(j):
        zt = jnp.where(z + j >= N_Z, z + j - N_Z, z + j)
        return pltpu.make_async_remote_copy(
            src_ref=ids1_send.at[zt],
            dst_ref=ids1_recv.at[z],
            send_sem=i1_send_sem,
            recv_sem=i1_recv_sem,
            device_id={"dp": zt * N_Y + y},
            device_id_type=MESH,
        )

    for j in Z_ORDER:
        ids1_copy(j).start()

    for other in others:
        block_copy(stats, other, sib, st_send_sem, st_recv_sem, 0).wait_recv()

    tops = [stats[b, :, 0:128] for b in range(N_GRP)]
    top = functools.reduce(jnp.maximum, tops)
    total = jnp.zeros((N_GRP, B_DEV), jnp.float32)
    for b in range(N_GRP):
        total = total + jnp.exp(tops[b] - top) * stats[b, :, 128:256]
    scale = jnp.exp(stats[g, :, 0:128] - top) / total
    pos_sub, pos_lane = iota((PER_ITEM, B_DEV), 0), iota((PER_ITEM, B_DEV), 1)
    for b in range(N_GRP):
        share = cross[b] * scale[b : b + 1]
        share = share - jnp.where(pos_sub + b * PER_ITEM == pos_lane + g * PER_ITEM, 1.0, 0.0)
        grads[:, b * B_DEV : (b + 1) * B_DEV] = (block_weights[b] * share).astype(jnp.bfloat16)
    item_grad = jnp.dot(
        grads[...], q_all[:, 0:B_DEV, :].reshape(N_GRP * B_DEV, D), preferred_element_type=jnp.float32
    ).astype(jnp.bfloat16)
    placed = jnp.dot(slots[...], item_grad, preferred_element_type=jnp.float32)
    send1[...] = placed.astype(jnp.bfloat16).reshape(N_Z, 2 * N_Y, D)

    def rows1_copy(j):
        zt = jnp.where(z + j >= N_Z, z + j - N_Z, z + j)
        return pltpu.make_async_remote_copy(
            src_ref=send1.at[zt],
            dst_ref=recv1.at[z],
            send_sem=r1_send_sem,
            recv_sem=r1_recv_sem,
            device_id={"dp": zt * N_Y + y},
            device_id_type=MESH,
        )

    for j in Z_ORDER:
        rows1_copy(j).start()
    recv1[z] = send1[z]

    def query_term(block):
        columns = pl.ds(pl.multiple_of(block * B_DEV, B_DEV), B_DEV)
        return tn_dot(grads[:, columns], items[...])

    def pair_copy(k):
        return pltpu.make_async_remote_copy(
            src_ref=dq_send.at[k],
            dst_ref=dq_got.at[k],
            send_sem=dp_send_sem.at[k],
            recv_sem=dp_recv_sem.at[k],
            device_id={"grp": sib},
            device_id_type=MESH,
        )

    for k in range(N_X):
        dq_send[k] = query_term(2 * chip(k) + 1 - c)
        pair_copy(k).start()
    for k in range(N_X):
        dq_keep[k] = query_term(2 * chip(k) + c)

    pltpu.make_async_copy(ids1_recv.at[pl.ds(0, N_Z - 1)], ids1_recv.at[pl.ds(0, N_Z - 1)], i1_recv_sem).wait()
    ids1_flat[...] = jnp.zeros((16, 128), jnp.float32)
    for k in range(N_Z):
        ids1_flat[k : k + 1, :] = ids1_recv[k]
    got1 = ids1_flat[...]
    y_sub, l_lane = iota((N_Y, 128), 0), iota((N_Y, 128), 1)
    z_sub, s_lane = iota((16, D), 0), iota((16, D), 1)
    ids2 = jnp.zeros((N_Y, D), jnp.float32)
    for k in range(2):
        pick = jnp.where(l_lane == 2 * y_sub + k, 1.0, 0.0)
        spread = jnp.where(s_lane == y * 32 + 2 * z_sub + k, 1.0, 0.0)
        picked = nt_dot(pick, got1, HIGHEST)
        ids2 = ids2 + jnp.dot(picked, spread, precision=HIGHEST, preferred_element_type=jnp.float32)
    summed = jnp.sum(got1, axis=0, keepdims=True)
    w_z = jnp.sum(jnp.where(iota((1, 128), 1) == 2 * N_Y, summed, 0.0), axis=1, keepdims=True)
    ids2 = jnp.where(iota((N_Y, D), 1) == y * 32 + 24, w_z, ids2)
    for k in range(N_Y):
        ids2_send[k] = ids2[k : k + 1]
    ids2_recv[y] = ids2_send[y]

    def ids2_copy(j):
        yt = jnp.where(y + j >= N_Y, y + j - N_Y, y + j)
        return pltpu.make_async_remote_copy(
            src_ref=ids2_send.at[yt],
            dst_ref=ids2_recv.at[y],
            send_sem=i2_send_sem,
            recv_sem=i2_recv_sem,
            device_id={"dp": z * N_Y + yt},
            device_id_type=MESH,
        )

    for j in Y_ORDER:
        ids2_copy(j).start()

    def chip_copy(k):
        return pltpu.make_async_remote_copy(
            src_ref=dq_terms.at[k],
            dst_ref=dq_in.at[k],
            send_sem=dx_send_sem.at[k],
            recv_sem=dx_recv_sem.at[k],
            device_id={"grp": 2 * chip(k) + c},
            device_id_type=MESH,
        )

    for k in (2, 1, 3):
        pair_copy(k).wait_recv()
        dq_terms[k] = (dq_keep[k] + dq_got[k]).astype(jnp.bfloat16)
        chip_copy(k).start()
    pair_copy(0).wait_recv()

    pltpu.make_async_copy(recv1.at[pl.ds(0, N_Z - 1)], recv1.at[pl.ds(0, N_Z - 1)], r1_recv_sem).wait()
    turned = jnp.dot(perm[...], recv1[...].reshape(2 * N_Z * N_Y, D), preferred_element_type=jnp.float32)
    send2[...] = turned.astype(jnp.bfloat16).reshape(N_Y, 32, D)

    def rows2_copy(j):
        yt = jnp.where(y + j >= N_Y, y + j - N_Y, y + j)
        return pltpu.make_async_remote_copy(
            src_ref=send2.at[yt],
            dst_ref=recv2.at[y],
            send_sem=r2_send_sem,
            recv_sem=r2_recv_sem,
            device_id={"dp": z * N_Y + yt},
            device_id_type=MESH,
        )

    for j in Y_ORDER:
        rows2_copy(j).start()
    recv2[y] = send2[y]

    pltpu.make_async_copy(ids2_recv.at[pl.ds(0, N_Y - 1)], ids2_recv.at[pl.ds(0, N_Y - 1)], i2_recv_sem).wait()
    got2 = ids2_recv[0]
    for k in range(1, N_Y):
        got2 = got2 + ids2_recv[k]
    in_block = iota((1, D), 1) % 32
    norm = BATCH / jnp.sum(jnp.where(in_block == 24, got2, 0.0), axis=1, keepdims=True)
    row_ids = jnp.where(in_block < 2 * N_Z, got2, 0.0).astype(jnp.int32)

    member[...] = jnp.where(iota((ROWS_DEV, D), 0) + 1 == row_ids, 1.0, 0.0).astype(jnp.bfloat16)
    query_grad = dq_keep[0] + dq_got[0]
    for k in (1, 3, 2):
        chip_copy(k).wait_recv()
        query_grad = query_grad + dq_in[k].astype(jnp.float32)
    dq_ref[...] = (query_grad * norm).astype(jnp.bfloat16)


    for copy in sent:
        copy.wait_send()
    for k in range(N_X):
        pair_copy(k).wait_send()
    for k in range(1, N_X):
        chip_copy(k).wait_send()
    for j in range(N_GRP - 1):
        stats_copy(j).wait_send()
    pltpu.make_async_copy(ids1_send.at[pl.ds(0, N_Z - 1)], ids1_send.at[pl.ds(0, N_Z - 1)], i1_send_sem).wait()
    pltpu.make_async_copy(ids2_send.at[pl.ds(0, N_Y - 1)], ids2_send.at[pl.ds(0, N_Y - 1)], i2_send_sem).wait()
    pltpu.make_async_copy(send1.at[pl.ds(0, N_Z - 1)], send1.at[pl.ds(0, N_Z - 1)], r1_send_sem).wait()
    pltpu.make_async_copy(recv2.at[pl.ds(0, N_Y - 1)], recv2.at[pl.ds(0, N_Y - 1)], r2_recv_sem).wait()
    rows_ref[...] = recv2[...].reshape(N_Y * 32, D)
    norm_ref[...] = jnp.broadcast_to(norm, (1, D))
    pltpu.make_async_copy(send2.at[pl.ds(0, N_Y - 1)], send2.at[pl.ds(0, N_Y - 1)], r2_send_sem).wait()


def write_out(query_ref, rows_ref, member_ref, norm_ref, dq_out, tab_out, table, dq_sem, tab_sems):
    query_copy = pltpu.make_async_copy(query_ref, dq_out, dq_sem)
    query_copy.start()
    size = ROWS_DEV // CHUNKS
    copies = []
    for k in range(CHUNKS):
        part = slice(k * size, (k + 1) * size)
        table[part, :] = norm_ref[...] * jnp.dot(
            member_ref[part, :], rows_ref[...], preferred_element_type=jnp.float32
        )
        copy = pltpu.make_async_copy(
            table.at[pl.ds(k * size, size)], tab_out.at[pl.ds(k * size, size)], tab_sems.at[k]
        )
        copy.start()
        copies.append(copy)
    query_copy.wait()
    for copy in copies:
        copy.wait()


def shards(queries, item_vecs, log_q, weights, item_owner, item_row):
    vmem = pl.BlockSpec(memory_space=pltpu.VMEM)
    bf16, f32 = jnp.bfloat16, jnp.float32
    dma = pltpu.SemaphoreType.DMA
    query_grad, rows, member, norm = pl.pallas_call(
        kernel,
        out_shape=(
            jax.ShapeDtypeStruct((B_DEV, D), bf16),
            jax.ShapeDtypeStruct((N_Y * 32, D), bf16),
            jax.ShapeDtypeStruct((ROWS_DEV, D), bf16),
            jax.ShapeDtypeStruct((1, D), f32),
        ),
        in_specs=[pl.BlockSpec(memory_space=pltpu.HBM)] * 6,
        out_specs=(vmem,) * 4,
        scratch_shapes=[
            pltpu.VMEM((PER_ITEM,), bf16),
            pltpu.VMEM((B_DEV,), bf16),
            pltpu.VMEM((1, PER_ITEM), jnp.int32),
            pltpu.VMEM((1, PER_ITEM), jnp.int32),
            pltpu.VMEM((PER_ITEM, D), bf16),
            pltpu.VMEM((N_GRP, Q_ROWS, D), bf16),
            pltpu.VMEM((N_GRP, PER_ITEM, B_DEV), f32),
            pltpu.VMEM((PER_ITEM, N_GRP * B_DEV), bf16),
            pltpu.VMEM((N_GRP, 1, 256), f32),
            pltpu.VMEM((N_GRP, N_GRP, 256), f32),
            pltpu.VMEM((N_X, B_DEV, D), f32),
            pltpu.VMEM((N_X, B_DEV, D), f32),
            pltpu.VMEM((N_X, B_DEV, D), f32),
            pltpu.VMEM((N_X, B_DEV, D), bf16),
            pltpu.VMEM((N_X, B_DEV, D), bf16),
            pltpu.VMEM((N_Z, 1, 128), f32),
            pltpu.VMEM((N_Z, 1, 128), f32),
            pltpu.VMEM((16, 128), f32),
            pltpu.VMEM((N_Y, 1, D), f32),
            pltpu.VMEM((N_Y, 1, D), f32),
            pltpu.VMEM((2 * N_Z * N_Y, PER_ITEM), bf16),
            pltpu.VMEM((N_Y * 32, 2 * N_Z * N_Y), bf16),
            pltpu.VMEM((N_Z, 2 * N_Y, D), bf16),
            pltpu.VMEM((N_Z, 2 * N_Y, D), bf16),
            pltpu.VMEM((N_Y, 32, D), bf16),
            pltpu.VMEM((N_Y, 32, D), bf16),
            dma((6,)), pltpu.SemaphoreType.REGULAR((2,)), pltpu.SemaphoreType.REGULAR,
            dma((7,)), dma((N_GRP,)),
            dma((N_GRP,)), dma((N_GRP,)),
            dma((N_X,)), dma((N_X,)), dma((N_X,)), dma((N_X,)),
            dma, dma, dma, dma, dma, dma, dma, dma,
        ],
        compiler_params=pltpu.CompilerParams(
            collective_id=0, has_side_effects=True, vmem_limit_bytes=32 * 1024 * 1024
        ),
    )(*(
        pltpu.with_memory_space_constraint(operand, pltpu.HBM)
        for operand in (
            queries,
            item_vecs,
            log_q,
            weights,
            item_owner.reshape(1, PER_ITEM),
            item_row.reshape(1, PER_ITEM),
        )
    ))
    hbm = pl.BlockSpec(memory_space=pl.ANY)
    return pl.pallas_call(
        write_out,
        out_shape=(
            jax.ShapeDtypeStruct((B_DEV, D), bf16),
            jax.ShapeDtypeStruct((ROWS_DEV, D), f32),
        ),
        in_specs=[vmem] * 4,
        out_specs=(hbm, hbm),
        scratch_shapes=[pltpu.VMEM((ROWS_DEV, D), f32), dma, dma((CHUNKS,))],
        compiler_params=pltpu.CompilerParams(vmem_limit_bytes=32 * 1024 * 1024),
    )(query_grad, rows, member, norm)


def solution(mesh):
    in_specs = (
        P(("grp", "dp"), None),
        P(("grp", "dp"), None),
        P(("grp", "dp")),
        P(("grp", "dp")),
        P(("grp", "dp"), None),
        P(("grp", "dp")),
    )
    out_specs = (P(("grp", "dp"), None), P(("grp", "dp"), None))
    return jax.shard_map(shards, mesh=mesh, in_specs=in_specs, out_specs=out_specs, check_vma=False)
```
